128 devices in a mesh: grp: 4 (over y), tile: 32 (over x, z, core).
Axes of the slice: x: 4, y: 4, z: 4, core: 2. Of those that a mesh axis runs over, the one named last changes fastest.
Arguments:
- flow_fields: float32 [5, 1024, 16, 128], P(None, 'tile', 'grp'), may hold values from -6 to 6
- turbulent_diffusivity: float32 [1024, 16, 128], P('tile', 'grp'), may hold values from 0.05 to 0.3
- holder_unit: int32 [4, 1024, 1], P('grp', 'tile'), may hold values from 0 to 31, as said below
- spray_volume_position: int32 [32, 1024, 128], P('tile'), may hold values from 0 to 511
- patch_pick_unreduced: int32 [32, 1024], P('tile'), may hold values from 0 to 1048575
- droplet_motion: float32 [32, 1024, 3, 128], P('tile'), may hold values from -6 to 6
- droplet_warmth: float32 [32, 1024, 128], P('tile'), may hold values from -6 to 6
- droplet_weightiness: float32 [32, 1024, 128], P('tile'), may hold values from 0.25 to 2
- droplet_multiplicity: float32 [32, 1024, 128], P('tile'), may hold values from 0.5 to 2
- living_spray_batches: int32 [32], P('tile'), may hold values from 1 to 1024, 16384 in all
Outputs:
- gas_next: float32 [5, 1024, 16, 128], P(None, 'tile', 'grp')
The draws below stay inside these ranges and needn't reach their ends.
Inputs may be any that keep to these rules, and one draw needn't show every extreme that they name: `holder_unit`: among the 32 tiles of one gas device (aligned blocks of 32 rows of owner, in order of its first two dimensions) no parcel device owns more than 2, and in every such block one parcel device owns exactly 2. Two parcel devices own no tile at all. Rows with g = 3 are not used. `living_spray_batches`: live blocks of a device are its first ones; the busiest parcel device has exactly 1024, and they sum to 16384.
All inputs are finite; a program needn't handle non-finite values.
Results may differ from the reference program's by a relative error of at most 0.0045.
Values may be sent and summed in bfloat16 or wider, within the bound.
No kernel may reach another device: no remote copies, remote signals or barrier semaphores. Data moves between devices by JAX's collectives and lax.ppermute only.
A program may use at most 64 MiB of HBM per device.

```python
import math
import jax
import jax.numpy as jnp
import numpy as np

NF = 5
GROUP_DROPLETS = 128
BY = 4
BZ = 128
BX = 32
UNIT_BATCHES = 1024
SPRAY_UNITS = 32
NX = 1024
NY = 16
GAS_Y = 12
SLOTS = 2
N_GRP = 4


def draw_holder_unit(key, part):
    block_count = NY // BY * (NX // BX)
    spare_count = SPRAY_UNITS - 2
    key_order, key_blocks, key_rows = jax.random.split(jax.random.fold_in(key, 7), 3)
    middle = (1 + jax.random.permutation(key_order, SPRAY_UNITS - 2)).astype(jnp.int32)
    allowed = jnp.concatenate([jnp.array([0, SPRAY_UNITS - 1], dtype=jnp.int32), middle[2:]])
    shuffles = jax.vmap(lambda subkey: jax.random.permutation(subkey, spare_count))(jax.random.split(key_blocks, block_count)).astype(jnp.int32)
    first_block = jnp.arange(block_count, dtype=jnp.int32)[:, None] == 0
    shuffles = jnp.where(first_block, jnp.arange(spare_count, dtype=jnp.int32)[None, :], shuffles)
    places = jnp.arange(BX, dtype=jnp.int32)
    column = jnp.where(places < SLOTS, 0, 1 + (places - SLOTS) % (spare_count - 1)).astype(jnp.int32)
    labels = allowed[jnp.take(shuffles, column, axis=1)]
    row_order = jax.vmap(lambda subkey: jax.random.permutation(subkey, BX))(jax.random.split(key_rows, block_count)).astype(jnp.int32)
    labels = jnp.take_along_axis(labels, row_order, axis=1)
    return labels.reshape(NY // BY, NX, 1).astype(jnp.int32)


def with_ends(entries, rng, low, high):
    index_at = [jax.random.randint(jax.random.fold_in(rng, axis), (), 0, length) for axis, length in enumerate(entries.shape)]
    widest = entries.shape.index(max(entries.shape))
    next_to = index_at[:widest] + [(index_at[widest] + 1) % entries.shape[widest]] + index_at[widest + 1:]
    return entries.at[tuple(index_at)].set(low).at[tuple(next_to)].set(high)


def shard_levels(rng, dims, cuts, least, high):
    loudness = 1.0
    for dim, shards_of in cuts:
        draws = jax.random.uniform(jax.random.fold_in(jax.random.fold_in(rng, 6), dim), (shards_of,), jnp.float32, least / len(cuts), high / len(cuts))
        loudness = loudness * jnp.repeat(jnp.exp(draws), dims[dim] // shards_of).reshape((-1,) + (1,) * (len(dims) - 1 - dim))
    return loudness


def split_up(amount, total, limit, skew):
    weights = [(1 << 20) // math.isqrt(rank ** skew) + 1 for rank in range(2, amount + 1)]
    rest, given = total - limit - (amount - 1), [1] * (amount - 1)
    while rest > 0:
        free = [i for i in range(amount - 1) if given[i] < limit]
        mass, budget = sum([weights[i] for i in free]), rest
        for i in free:
            extra = min(limit - given[i], max(1, budget * weights[i] // mass), rest)
            given[i] = given[i] + extra
            rest = rest - extra
    return np.array([limit] + given)


def uneven(stream_key, count, total, reach, skew):
    if count == 2:
        one = jax.random.randint(stream_key, (), max(1, total - reach), min(reach, total - 1) + 1)
        return jnp.stack([one, total - one])
    tallies = jnp.asarray(split_up(count, total, reach, skew), jnp.int32)
    twos = (count - 1) // 2
    source_of, receiver = tallies[1:1 + 2 * twos:2], tallies[2:2 + 2 * twos:2]
    margin = jnp.minimum(source_of - 1, reach - receiver)
    passed = jax.random.randint(jax.random.fold_in(stream_key, 1), (twos,), 0, 1 << 20) % (margin + 1)
    tallies = tallies.at[1:1 + 2 * twos:2].set(source_of - passed).at[2:2 + 2 * twos:2].set(receiver + passed)
    return tallies[jax.random.permutation(jax.random.fold_in(stream_key, 2), count)]


def scatter_about(key, shape, scale, bound, pieces=(), kind=jnp.bfloat16):
    level = shard_levels(key, shape, pieces, -0.22, 0.18) if pieces else 1.0
    drawn = jax.random.normal(key, shape, jnp.float32) * scale * level
    return jnp.minimum(jnp.maximum(drawn, -bound), bound).astype(kind)


def setup_inputs(seed: int = 0) -> dict:
    keys = jax.random.split(jax.random.key(seed), 11)
    flow_fields = scatter_about(keys[0], (NF, NX, NY, BZ), 1.0, 6.0, ((1, 32), (2, 4)), jnp.float32)
    turbulent_diffusivity = jnp.clip(jnp.exp(math.log(0.3) - 1.7917595 * jax.random.uniform(keys[1], (NX, NY, BZ), jnp.float32) ** shard_levels(keys[1], (NX, NY, BZ), ((0, 32), (1, 4)), -0.2, 0.2)), 0.05, 0.3)
    holder_unit = draw_holder_unit(jax.random.fold_in(keys[10], 71), 0)
    spray_volume_position = with_ends(jax.random.randint(keys[3], (SPRAY_UNITS, UNIT_BATCHES, GROUP_DROPLETS), 0, BY * BZ), jax.random.fold_in(keys[3], 1), 0, (BY * BZ) - 1).astype(jnp.int32)
    patch_pick_unreduced = with_ends(jax.random.randint(keys[4], (SPRAY_UNITS, UNIT_BATCHES), 0, 1048576), jax.random.fold_in(keys[4], 1), 0, 1048575).astype(jnp.int32)
    droplet_motion = scatter_about(keys[5], (SPRAY_UNITS, UNIT_BATCHES, 3, GROUP_DROPLETS), 1.0, 6.0, ((0, 32),), jnp.float32)
    droplet_warmth = scatter_about(keys[6], (SPRAY_UNITS, UNIT_BATCHES, GROUP_DROPLETS), 1.0, 6.0, ((0, 32),), jnp.float32)
    droplet_weightiness = jnp.clip(jnp.exp(math.log(2.0) - 2.0794415 * jax.random.uniform(keys[7], (SPRAY_UNITS, UNIT_BATCHES, GROUP_DROPLETS), jnp.float32) ** shard_levels(keys[7], (SPRAY_UNITS, UNIT_BATCHES, GROUP_DROPLETS), ((0, 32),), -0.2, 0.2)), 0.25, 2.0)
    droplet_multiplicity = jnp.clip(jnp.exp(math.log(2.0) - 1.3862944 * jax.random.uniform(keys[8], (SPRAY_UNITS, UNIT_BATCHES, GROUP_DROPLETS), jnp.float32) ** shard_levels(keys[8], (SPRAY_UNITS, UNIT_BATCHES, GROUP_DROPLETS), ((0, 32),), -0.2, 0.2)), 0.5, 2.0)
    living_spray_batches = uneven(keys[9], SPRAY_UNITS, SPRAY_UNITS * UNIT_BATCHES // 2, UNIT_BATCHES, 2).astype(jnp.int32)
    return dict(flow_fields=flow_fields, turbulent_diffusivity=turbulent_diffusivity, holder_unit=holder_unit, spray_volume_position=spray_volume_position, patch_pick_unreduced=patch_pick_unreduced, droplet_motion=droplet_motion, droplet_warmth=droplet_warmth, droplet_weightiness=droplet_weightiness, droplet_multiplicity=droplet_multiplicity, living_spray_batches=living_spray_batches)


def droplet_coupling_feeds(reached_markers, droplet_motion, droplet_warmth, droplet_weightiness, droplet_multiplicity):
    gas_velocity = reached_markers[..., 0:3, :]
    fluid_warming_share = reached_markers[..., 3, :]
    gas_fuel = reached_markers[..., 4, :]
    relative = gas_velocity - droplet_motion
    speed_sq = jnp.sum(relative * relative, axis=-2)
    surface = droplet_weightiness ** (2.0 / 3.0)
    inverse_tau = 0.8 * (1.0 + 0.15 * (1.0 + speed_sq) ** 0.3435) / surface
    relaxation = 1.0 - jnp.exp(-0.5 * inverse_tau)
    new_velocity = droplet_motion + relaxation[..., None, :] * relative
    heating = 1.0 / (1.0 + jnp.exp(-(fluid_warming_share - gas_fuel)))
    leftover_liquid_load = jnp.exp(-0.3 * heating / surface)
    updated_droplet_load = droplet_weightiness * leftover_liquid_load
    warming_speed = 1.0 - jnp.exp(-0.25 * inverse_tau)
    updated_droplet_warmth = droplet_warmth + warming_speed * (fluid_warming_share - droplet_warmth) - 0.5 * (1.0 - leftover_liquid_load)
    momentum = droplet_weightiness[..., None, :] * droplet_motion - updated_droplet_load[..., None, :] * new_velocity
    enthalpy_content = droplet_weightiness * droplet_warmth - updated_droplet_load * updated_droplet_warmth
    stacked = jnp.concatenate([momentum, enthalpy_content[..., None, :], (droplet_weightiness - updated_droplet_load)[..., None, :]], axis=-2)
    return droplet_multiplicity[..., None, :] * stacked


def reference(flow_fields, turbulent_diffusivity, holder_unit, spray_volume_position, patch_pick_unreduced, droplet_motion, droplet_warmth, droplet_weightiness, droplet_multiplicity, living_spray_batches):
    gas_rows = GAS_Y
    groups = N_GRP - 1
    tile_cells = BY * BZ
    gas_field = flow_fields[:, :, :gas_rows, :]
    nu_field = turbulent_diffusivity[:, :gas_rows, :]
    padded = jnp.pad(gas_field, ((0, 0), (1, 1), (1, 1), (1, 1)))
    beside = padded[:, 2:, 1:-1, 1:-1] + padded[:, :-2, 1:-1, 1:-1]
    beside = beside + padded[:, 1:-1, 2:, 1:-1] + padded[:, 1:-1, :-2, 1:-1]
    beside = beside + padded[:, 1:-1, 1:-1, 2:] + padded[:, 1:-1, 1:-1, :-2]
    laplace = beside - 6.0 * gas_field
    tiles = gas_field.astype(jnp.bfloat16).reshape(NF, NX, groups, BY, BZ)
    tiles = tiles.transpose(2, 1, 0, 3, 4).reshape(groups * NX, NF, tile_cells)
    plane_owner = holder_unit[:groups, :, 0].reshape(groups * NX)
    owned = plane_owner[None, :] == jnp.arange(SPRAY_UNITS, dtype=jnp.int32)[:, None]
    owned_count = jnp.sum(owned.astype(jnp.int32), axis=1)
    listing = jnp.argsort(jnp.where(owned, 0, 1).astype(jnp.int32), axis=1, stable=True).astype(jnp.int32)
    picked = (patch_pick_unreduced % jnp.maximum(owned_count, 1)[:, None]).astype(jnp.int32)
    block_tile = jnp.take_along_axis(listing, picked, axis=1)
    alive = (jnp.arange(UNIT_BATCHES, dtype=jnp.int32)[None, :] < living_spray_batches[:, None]) & (owned_count[:, None] > 0)
    reached_markers = tiles[block_tile[:, :, None], :, spray_volume_position].astype(jnp.float32).transpose(0, 1, 3, 2)
    coupling_feeds = droplet_coupling_feeds(reached_markers, droplet_motion, droplet_warmth, droplet_weightiness, droplet_multiplicity)
    coupling_feeds = coupling_feeds * alive[:, :, None, None].astype(jnp.float32)
    deposit = jnp.zeros((groups * NX, NF, tile_cells), jnp.float32)
    deposit = deposit.at[block_tile[:, :, None], :, spray_volume_position].add(coupling_feeds.transpose(0, 1, 3, 2))
    placed = deposit.reshape(groups, NX, NF, BY, BZ).transpose(2, 1, 0, 3, 4).reshape(NF, NX, gas_rows, BZ)
    advanced = gas_field + 0.5 * nu_field * laplace + placed
    return jnp.concatenate([advanced, jnp.zeros((NF, NX, BY, BZ), jnp.float32)], axis=2)
```

```python
import jax
import jax.numpy as jnp
from jax import lax
from jax.experimental import pallas as pl
from jax.experimental.pallas import tpu as pltpu
from jax.sharding import PartitionSpec as P

NF = 5
ROWS_Y = 4
LANES = 128
PAIR = 48
HALF = NF * ROWS_Y
VMEM_LIMIT = 48 * 1024 * 1024
NT = (((1,), (1,)), ((), ()))


def pack_kernel(planes, owners, holder_ref, near_refs, flow_ref, out_ref, plane_of, count):
    g = lax.axis_index("grp")
    groups = lax.axis_size("grp")

    def clear(p, carry):
        count[p] = 0
        plane_of[2 * p] = 0
        plane_of[2 * p + 1] = 0
        return carry

    lax.fori_loop(0, owners, clear, 0, unroll=True)

    def place(x, carry):
        owner = holder_ref[x]
        rank = count[owner]
        plane_of[2 * owner + jnp.minimum(rank, 1)] = x
        count[owner] = rank + 1
        return carry

    lax.fori_loop(0, planes, place, 0, unroll=True)

    owner_ids = lax.broadcasted_iota(jnp.int32, (owners, planes), 0)
    own = jnp.zeros((owners, 1), jnp.float32)
    before = jnp.zeros((owners, 1), jnp.float32)
    total = jnp.zeros((owners, 1), jnp.float32)
    for k, ref in enumerate(near_refs):
        group = (g - k + groups) % groups
        hits = jnp.where(owner_ids == ref[...], 1.0, 0.0)
        tally = jnp.sum(hits, axis=1, keepdims=True)
        tally = jnp.where(group < groups - 1, tally, 0.0)
        total = total + tally
        before = before + jnp.where(group < g, tally, 0.0)
        if k == 0:
            own = tally
    own, before, total = (jnp.broadcast_to(v, (owners, LANES)) for v in (own, before, total))
    row = lax.broadcasted_iota(jnp.int32, (8, LANES), 0)
    for p in range(owners):
        flags = jnp.where(
            row == 0,
            own[p : p + 1],
            jnp.where(row == 1, before[p : p + 1], jnp.where(row == 2, total[p : p + 1], 0.0)),
        )
        pieces = []
        for s in range(2):
            x = plane_of[2 * p + s]
            pieces += [flow_ref[f, x] for f in range(NF)]
        out_ref[p] = jnp.concatenate(pieces + [flags], axis=0).astype(jnp.bfloat16)


def slot_relayout():
    r = lax.broadcasted_iota(jnp.int32, (64, PAIR), 0)
    c = lax.broadcasted_iota(jnp.int32, (64, PAIR), 1)
    f = r & 7
    want = (r >> 5) * HALF + f * ROWS_Y + ((r >> 3) & 3)
    return jnp.where((f < NF) & (c == want), 1.0, 0.0).astype(jnp.bfloat16)


def slot_relayout_back():
    r = lax.broadcasted_iota(jnp.int32, (PAIR, 64), 0)
    c = lax.broadcasted_iota(jnp.int32, (PAIR, 64), 1)
    f = c & 7
    want = (c >> 5) * HALF + f * ROWS_Y + ((c >> 3) & 3)
    return jnp.where((f < NF) & (r == want), 1.0, 0.0).astype(jnp.bfloat16)


def coupling(gas, motion, warmth, mass, weight):
    relative = [gas[k] - motion[k] for k in range(3)]
    speed_sq = relative[0] * relative[0] + relative[1] * relative[1] + relative[2] * relative[2]
    inv_surface = jnp.exp((-2.0 / 3.0) * jnp.log(mass))
    drag = 0.8 * (1.0 + 0.15 * jnp.exp(0.3435 * jnp.log(1.0 + speed_sq)))
    inverse_tau = drag * inv_surface
    relaxation = 1.0 - jnp.exp(-0.5 * inverse_tau)
    heating = 1.0 / (1.0 + jnp.exp(gas[4] - gas[3]))
    remain = jnp.exp(-0.3 * heating * inv_surface)
    new_mass = mass * remain
    warming = 1.0 - jnp.exp(-0.25 * inverse_tau)
    new_warmth = warmth + warming * (gas[3] - warmth) - 0.5 * (1.0 - remain)
    out = []
    for k in range(3):
        new_velocity = motion[k] + relaxation * relative[k]
        out.append(weight * (mass * motion[k] - new_mass * new_velocity))
    out.append(weight * (mass * warmth - new_mass * new_warmth))
    out.append(weight * (mass - new_mass))
    return out


def couple_kernel(
    owners,
    blocks,
    live_ref,
    pick_ref,
    recv_ref,
    cell_hbm,
    motion_hbm,
    warmth_hbm,
    mass_hbm,
    weight_hbm,
    out_ref,
    cell,
    motion,
    warmth,
    mass,
    weight,
    table,
    deposit,
    code_v,
    code_s,
    work,
    seen,
    gathered,
    source,
    sems,
):
    slots = 2 * owners
    copies = [
        pltpu.make_async_copy(a, b, sems.at[i])
        for i, (a, b) in enumerate(
            (
                (cell_hbm, cell),
                (motion_hbm, motion),
                (warmth_hbm, warmth),
                (mass_hbm, mass),
                (weight_hbm, weight),
            )
        )
    ]
    for copy in copies:
        copy.start()

    before = jnp.zeros((8, LANES), jnp.float32)
    total = jnp.zeros((8, LANES), jnp.float32)
    counts = []
    for t in range(owners):
        flags = recv_ref[t, 32:48].astype(jnp.float32)
        counts.append(jnp.broadcast_to(flags[8:9], (8, LANES)))
        before = before + jnp.broadcast_to(flags[9:10], (8, LANES))
        total = total + jnp.broadcast_to(flags[10:11], (8, LANES))
    divisor = jnp.maximum(total, 1.0)
    pick = pick_ref[...].astype(jnp.float32)
    quotient = (pick / divisor).astype(jnp.int32)
    divisor_int = divisor.astype(jnp.int32)
    picked = pick_ref[...] - quotient * divisor_int
    picked = jnp.where(picked < 0, picked + divisor_int, picked)
    picked = jnp.where(picked >= divisor_int, picked - divisor_int, picked)
    place = picked.astype(jnp.float32) - before
    running = jnp.zeros((8, LANES), jnp.float32)
    passed = jnp.zeros((8, LANES), jnp.float32)
    slot = jnp.zeros((8, LANES), jnp.float32)
    for t in range(owners):
        running = running + counts[t]
        beyond = running <= place
        slot = jnp.where(beyond, slot + 2.0, slot)
        passed = jnp.where(beyond, running, passed)
    slot = (slot + (place - passed)).astype(jnp.int32)
    block = (
        lax.broadcasted_iota(jnp.int32, (8, LANES), 0) * LANES
        + lax.broadcasted_iota(jnp.int32, (8, LANES), 1)
    )
    mine = (place >= 0.0) & (place < running) & (block < live_ref[0])
    code_v[...] = jnp.where(mine, slot * blocks + block, -1)
    to_scalar = pltpu.make_async_copy(code_v, code_s, sems.at[5])
    to_scalar.start()

    spread = slot_relayout()
    for t in range(owners):
        rows = jnp.dot(spread, recv_ref[t], preferred_element_type=jnp.float32)
        table[8 * t : 8 * t + 8] = rows.reshape(8, 8, LANES)
    table[4 * slots : 4 * slots + 4] = jnp.zeros((4, 8, LANES), jnp.float32)

    def clear(t, carry):
        deposit[pl.ds(8 * t, 8)] = jnp.zeros((8, 8, LANES), jnp.float32)
        return carry

    lax.fori_loop(0, owners, clear, 0)
    deposit[4 * slots : 4 * slots + 4] = jnp.zeros((4, 8, LANES), jnp.float32)
    source[...] = jnp.zeros_like(source)
    to_scalar.wait()

    def collect(j, n):
        for i in range(8):
            code = code_s[j >> 4, (j & 15) * 8 + i]
            work[n] = code
            n = n + jnp.where(code >= 0, 1, 0)
        return n

    found = lax.fori_loop(0, (live_ref[0] + 7) // 8, collect, 0)
    for i in range(8):
        work[found + i] = slots * blocks
    for copy in copies:
        copy.wait()

    cell_row = lax.broadcasted_iota(jnp.int32, (LANES, LANES), 0)

    def advance(j, carry):
        where_to = []
        for i in range(8):
            code = work[8 * j + i]
            b = code & (blocks - 1)
            slot = code >> (blocks.bit_length() - 1)
            cells = cell[pl.ds(b, 1), :]
            where_to.append((slot, cells))
            around = jnp.broadcast_to(cells, (8, LANES))
            z, y = around & (LANES - 1), around >> 7
            rows = [
                jnp.take_along_axis(table[4 * slot + k], z, axis=1) for k in range(ROWS_Y)
            ]
            seen[8 * i : 8 * i + 8] = jnp.where(
                y == 0, rows[0], jnp.where(y == 1, rows[1], jnp.where(y == 2, rows[2], rows[3]))
            )
            moving = motion[b]
            for k in range(3):
                gathered[k, i : i + 1, :] = moving[k : k + 1]
            gathered[3, i : i + 1, :] = warmth[pl.ds(b, 1), :]
            gathered[4, i : i + 1, :] = mass[pl.ds(b, 1), :]
            gathered[5, i : i + 1, :] = weight[pl.ds(b, 1), :]
        gas = [seen[pl.ds(f, 8, stride=8), :] for f in range(NF)]
        sources = coupling(
            gas, [gathered[k] for k in range(3)], gathered[3], gathered[4], gathered[5]
        )
        for f in range(NF):
            source[pl.ds(f, 8, stride=8), :] = sources[f]
        for i in range(8):
            slot, cells = where_to[i]
            around = jnp.broadcast_to(cells, (8, LANES))
            y = around >> 7
            part = source[8 * i : 8 * i + 8]
            masked = jnp.concatenate([jnp.where(y == k, part, 0.0) for k in range(ROWS_Y)], axis=0)
            upper = masked.astype(jnp.bfloat16)
            lower = (masked - upper.astype(jnp.float32)).astype(jnp.bfloat16)
            hot = jnp.where(cell_row == (cells & (LANES - 1)), 1.0, 0.0).astype(jnp.bfloat16)
            both = lax.dot_general(
                jnp.concatenate([upper, lower], axis=0), hot, NT, preferred_element_type=jnp.float32
            )
            added = (both[:32] + both[32:]).reshape(4, 8, LANES)
            deposit[pl.ds(4 * slot, 4)] = deposit[pl.ds(4 * slot, 4)] + added
        return carry

    lax.fori_loop(0, (found + 7) // 8, advance, 0)

    back = slot_relayout_back()
    for t in range(owners):
        rows = deposit[8 * t : 8 * t + 8].reshape(64, LANES).astype(jnp.bfloat16)
        out_ref[t] = jnp.dot(back, rows, preferred_element_type=jnp.float32).astype(jnp.bfloat16)


def diffuse_kernel(planes, flow_ref, nu_ref, xlo_ref, xhi_ref, ylo_ref, yhi_ref, out_ref):
    lane = lax.broadcasted_iota(jnp.int32, (ROWS_Y, LANES), 1)
    for f in range(NF):
        for x in range(planes):
            here = flow_ref[f, x]
            left = xlo_ref[f] if x == 0 else flow_ref[f, x - 1]
            right = xhi_ref[f] if x == planes - 1 else flow_ref[f, x + 1]
            lower = jnp.concatenate([ylo_ref[f, x : x + 1], here[: ROWS_Y - 1]], axis=0)
            upper = jnp.concatenate([here[1:], yhi_ref[f, x : x + 1]], axis=0)
            back = jnp.where(lane == 0, 0.0, pltpu.roll(here, 1, 1))
            ahead = jnp.where(lane == LANES - 1, 0.0, pltpu.roll(here, LANES - 1, 1))
            laplace = right + left + upper + lower + ahead + back - 6.0 * here
            out_ref[f, x] = here + 0.5 * nu_ref[x] * laplace


def finish_kernel(planes, owners, holder_ref, adv_ref, recv_ref, out_ref, count):
    g = lax.axis_index("grp")
    keep = g < lax.axis_size("grp") - 1

    def clear(p, carry):
        count[p] = 0
        return carry

    lax.fori_loop(0, owners, clear, 0, unroll=True)
    for x in range(planes):
        owner = holder_ref[x]
        rank = count[owner]
        count[owner] = rank + 1
        pair = recv_ref[owner].astype(jnp.float32)
        landed = jnp.where(rank == 0, pair[:HALF], pair[HALF : 2 * HALF])
        for f in range(NF):
            value = adv_ref[f, x] + landed[ROWS_Y * f : ROWS_Y * f + ROWS_Y]
            out_ref[f, x] = jnp.where(keep, value, 0.0)


def local(
    flow_fields,
    turbulent_diffusivity,
    holder_unit,
    spray_volume_position,
    patch_pick_unreduced,
    droplet_motion,
    droplet_warmth,
    droplet_weightiness,
    droplet_multiplicity,
    living_spray_batches,
):
    groups = lax.axis_size("grp")
    owners = lax.axis_size("tile")
    planes = flow_fields.shape[1]
    blocks = spray_volume_position.shape[1]
    vmem = pl.BlockSpec(memory_space=pltpu.VMEM)
    smem = pl.BlockSpec(memory_space=pltpu.SMEM)
    hbm = pl.BlockSpec(memory_space=pl.ANY)
    params = pltpu.CompilerParams(vmem_limit_bytes=VMEM_LIMIT)

    holder = holder_unit.reshape(planes)
    near = [holder.reshape(1, planes)]
    for k in range(1, groups):
        near.append(lax.ppermute(near[0], "grp", [(i, (i + k) % groups) for i in range(groups)]))

    up_tile = [(i, i + 1) for i in range(owners - 1)]
    up_grp = [(i, i + 1) for i in range(groups - 2)]
    xlo = lax.ppermute(flow_fields[:, planes - 1], "tile", up_tile)
    xhi = lax.ppermute(flow_fields[:, 0], "tile", [(b, a) for a, b in up_tile])
    ylo = lax.ppermute(flow_fields[:, :, ROWS_Y - 1], "grp", up_grp)
    yhi = lax.ppermute(flow_fields[:, :, 0], "grp", [(b, a) for a, b in up_grp])

    def pack_body(holder_ref, n0, n1, n2, n3, flow_ref, out_ref, plane_of, count):
        pack_kernel(
            planes, owners, holder_ref, (n0, n1, n2, n3), flow_ref, out_ref, plane_of, count
        )

    message = jax.ShapeDtypeStruct((owners, PAIR, LANES), jnp.bfloat16)
    packed = pl.pallas_call(
        pack_body,
        out_shape=message,
        in_specs=[smem] + [vmem] * 5,
        out_specs=vmem,
        scratch_shapes=[pltpu.SMEM((2 * owners,), jnp.int32), pltpu.SMEM((owners,), jnp.int32)],
        compiler_params=params,
    )(holder, *near, flow_fields)
    arrived = lax.all_to_all(packed, "tile", 0, 0, tiled=True)

    def couple_body(*refs):
        couple_kernel(owners, blocks, *refs)

    outgoing = pl.pallas_call(
        couple_body,
        out_shape=message,
        in_specs=[smem, vmem, vmem] + [hbm] * 5,
        out_specs=vmem,
        scratch_shapes=[
            pltpu.VMEM((blocks, LANES), jnp.int32),
            pltpu.VMEM((blocks, 3, LANES), jnp.float32),
            pltpu.VMEM((blocks, LANES), jnp.float32),
            pltpu.VMEM((blocks, LANES), jnp.float32),
            pltpu.VMEM((blocks, LANES), jnp.float32),
            pltpu.VMEM((8 * owners + 4, 8, LANES), jnp.float32),
            pltpu.VMEM((8 * owners + 4, 8, LANES), jnp.float32),
            pltpu.VMEM((8, LANES), jnp.int32),
            pltpu.SMEM((8, LANES), jnp.int32),
            pltpu.SMEM((blocks + 16,), jnp.int32),
            pltpu.VMEM((64, LANES), jnp.float32),
            pltpu.VMEM((6, 8, LANES), jnp.float32),
            pltpu.VMEM((64, LANES), jnp.float32),
            pltpu.SemaphoreType.DMA((6,)),
        ],
        compiler_params=params,
    )(
        living_spray_batches,
        patch_pick_unreduced.reshape(8, LANES),
        arrived,
        spray_volume_position[0],
        droplet_motion[0],
        droplet_warmth[0],
        droplet_weightiness[0],
        droplet_multiplicity[0],
    )
    landed = lax.all_to_all(outgoing, "tile", 0, 0, tiled=True)

    def diffuse_body(*refs):
        diffuse_kernel(planes, *refs)

    diffused = pl.pallas_call(
        diffuse_body,
        out_shape=jax.ShapeDtypeStruct(flow_fields.shape, jnp.float32),
        in_specs=[vmem] * 6,
        out_specs=vmem,
        compiler_params=params,
    )(flow_fields, turbulent_diffusivity, xlo, xhi, ylo, yhi)

    def finish_body(*refs):
        finish_kernel(planes, owners, *refs)

    return pl.pallas_call(
        finish_body,
        out_shape=jax.ShapeDtypeStruct(flow_fields.shape, jnp.float32),
        in_specs=[smem, vmem, vmem],
        out_specs=vmem,
        scratch_shapes=[pltpu.SMEM((owners,), jnp.int32)],
        compiler_params=params,
    )(holder, diffused, landed)


def solution(mesh):
    in_specs = (
        P(None, "tile", "grp", None),
        P("tile", "grp", None),
        P("grp", "tile", None),
        P("tile", None, None),
        P("tile", None),
        P("tile", None, None, None),
        P("tile", None, None),
        P("tile", None, None),
        P("tile", None, None),
        P("tile"),
    )
    out_specs = P(None, "tile", "grp", None)
    return jax.shard_map(local, mesh=mesh, in_specs=in_specs, out_specs=out_specs, check_vma=False)
```

```python
import jax
import jax.numpy as jnp
from jax import lax
from jax.experimental import pallas as pl
from jax.experimental.pallas import tpu as pltpu
from jax.sharding import PartitionSpec as P

NF = 5
ROWS_Y = 4
LANES = 128
PAIR = 48
HALF = NF * ROWS_Y
VMEM_LIMIT = 48 * 1024 * 1024
COUPLE_VMEM = 62 * 1024 * 1024
NT = (((1,), (1,)), ((), ()))


def pack_kernel(planes, owners, holder_ref, own_ref, up_ref, down_ref, flow_ref, out_ref, plane_of, count):
    g = lax.axis_index("grp")
    gas_groups = lax.axis_size("grp") - 1

    def clear(p, carry):
        count[p] = 0
        plane_of[2 * p] = 0
        plane_of[2 * p + 1] = 0
        return carry

    lax.fori_loop(0, owners, clear, 0, unroll=True)

    def place(x, carry):
        owner = holder_ref[x]
        rank = count[owner]
        plane_of[2 * owner + jnp.minimum(rank, 1)] = x
        count[owner] = rank + 1
        return carry

    lax.fori_loop(0, planes, place, 0, unroll=True)

    owner_ids = lax.broadcasted_iota(jnp.int32, (owners, planes), 0)

    def tally(ref):
        hits = jnp.where(owner_ids == ref[...], 1.0, 0.0)
        return jnp.broadcast_to(jnp.sum(hits, axis=1, keepdims=True), (owners, LANES))

    own = jnp.where(g < gas_groups, tally(own_ref), 0.0)
    above = tally(up_ref)
    below = tally(down_ref)
    total = own + above + below
    before = jnp.where(g >= 1, above, 0.0) + jnp.where(g == gas_groups - 1, below, 0.0)
    row = lax.broadcasted_iota(jnp.int32, (8, LANES), 0)
    for p in range(owners):
        flags = jnp.where(
            row == 0,
            own[p : p + 1],
            jnp.where(row == 1, before[p : p + 1], jnp.where(row == 2, total[p : p + 1], 0.0)),
        )
        pieces = []
        for s in range(2):
            x = plane_of[2 * p + s]
            pieces += [flow_ref[f, x] for f in range(NF)]
        out_ref[p] = jnp.concatenate(pieces + [flags], axis=0).astype(jnp.bfloat16)


def slot_relayout():
    r = lax.broadcasted_iota(jnp.int32, (64, PAIR), 0)
    c = lax.broadcasted_iota(jnp.int32, (64, PAIR), 1)
    f = r & 7
    want = (r >> 5) * HALF + f * ROWS_Y + ((r >> 3) & 3)
    return jnp.where((f < NF) & (c == want), 1.0, 0.0).astype(jnp.bfloat16)


def slot_relayout_back():
    r = lax.broadcasted_iota(jnp.int32, (PAIR, 64), 0)
    c = lax.broadcasted_iota(jnp.int32, (PAIR, 64), 1)
    f = c & 7
    want = (c >> 5) * HALF + f * ROWS_Y + ((c >> 3) & 3)
    return jnp.where((f < NF) & (r == want), 1.0, 0.0).astype(jnp.bfloat16)


def coupling(gas, motion, warmth, mass, weight):
    relative = [gas[k] - motion[k] for k in range(3)]
    speed_sq = relative[0] * relative[0] + relative[1] * relative[1] + relative[2] * relative[2]
    inv_surface = jnp.exp((-2.0 / 3.0) * jnp.log(mass))
    drag = 0.8 * (1.0 + 0.15 * jnp.exp(0.3435 * jnp.log(1.0 + speed_sq)))
    inverse_tau = drag * inv_surface
    relaxation = 1.0 - jnp.exp(-0.5 * inverse_tau)
    heating = 1.0 / (1.0 + jnp.exp(gas[4] - gas[3]))
    remain = jnp.exp(-0.3 * heating * inv_surface)
    new_mass = mass * remain
    warming = 1.0 - jnp.exp(-0.25 * inverse_tau)
    new_warmth = warmth + warming * (gas[3] - warmth) - 0.5 * (1.0 - remain)
    out = []
    for k in range(3):
        new_velocity = motion[k] + relaxation * relative[k]
        out.append(weight * (mass * motion[k] - new_mass * new_velocity))
    out.append(weight * (mass * warmth - new_mass * new_warmth))
    out.append(weight * (mass - new_mass))
    return out


UA, UB, UC = 32, 32, 32
ENTRY_BITS = 11
ENTRY = 1 << ENTRY_BITS


def ordered_by_slot(slot, slots):
    lanes = slot.shape[1]
    spare = slots * ENTRY + slot.shape[0] * lanes
    slot_row = lax.broadcasted_iota(jnp.int32, (slots, lanes), 0)
    hits = [slot_row == jnp.broadcast_to(slot[r : r + 1], (slots, lanes)) for r in range(8)]
    p = lax.broadcasted_iota(jnp.int32, (lanes, 2 * lanes), 0)
    q = lax.broadcasted_iota(jnp.int32, (lanes, 2 * lanes), 1)
    upto = jnp.where(p <= q, 1.0, 0.0).astype(jnp.bfloat16)
    ones = jnp.concatenate([jnp.where(h, 1.0, 0.0).astype(jnp.bfloat16) for h in hits], axis=0)
    tally = jnp.dot(ones, upto, preferred_element_type=jnp.float32)
    count = sum(tally[slots * r : slots * (r + 1), lanes:] for r in range(8))
    pairs = ((count.astype(jnp.int32) + 1) >> 1)
    p = lax.broadcasted_iota(jnp.int32, (slots, slots), 0)
    q = lax.broadcasted_iota(jnp.int32, (slots, slots), 1)
    before = jnp.where(q < p, 1.0, 0.0).astype(jnp.bfloat16)
    halves = jnp.concatenate([(pairs >> 4).astype(jnp.float32), (pairs & 15).astype(jnp.float32)], axis=1)
    ahead = jnp.dot(before, halves.astype(jnp.bfloat16), preferred_element_type=jnp.float32)
    start = 2.0 * (16.0 * ahead[:, :lanes] + ahead[:, lanes:])
    number = start[slots - 1 :].astype(jnp.int32) + 2 * pairs[slots - 1 :]
    carry = start - 1.0
    low = lax.broadcasted_iota(jnp.int32, (lanes, lanes), 0)
    high = lax.broadcasted_iota(jnp.int32, (16, lanes), 0)
    lane = lax.broadcasted_iota(jnp.int32, (16, lanes), 1).astype(jnp.float32)
    values, places = [], []
    for r in range(8):
        here = tally[slots * r : slots * (r + 1)]
        at = jnp.sum(jnp.where(hits[r], here[:, :lanes] + carry, 0.0), axis=0, keepdims=True)
        carry = carry + here[:, lanes:]
        own = slot[r : r + 1]
        at = jnp.where(own >= 0, at.astype(jnp.int32), -1)
        mask = high == (at >> 7)
        for_own = jnp.broadcast_to(own.astype(jnp.float32), (16, lanes))
        values.append(
            jnp.concatenate(
                [jnp.where(mask, v, 0.0) for v in (1.0, float(r), lane, for_own)], axis=0
            ).astype(jnp.bfloat16)
        )
        places.append(jnp.where(low == (at & (lanes - 1)), 1.0, 0.0).astype(jnp.bfloat16))
    found = lax.dot_general(
        jnp.concatenate(values, axis=1),
        jnp.concatenate(places, axis=1),
        NT,
        preferred_element_type=jnp.float32,
    )
    code = found[48:64] * float(ENTRY) + found[16:32] * float(lanes) + found[32:48]
    code = jnp.where(found[:16] > 0.5, code.astype(jnp.int32), spare)
    return jnp.where(high == 15, jnp.broadcast_to(number, (16, lanes)), code)


def couple_kernel(
    owners,
    blocks,
    live_ref,
    pick_ref,
    recv_ref,
    cell_hbm,
    motion_hbm,
    warmth_hbm,
    mass_hbm,
    weight_hbm,
    out_ref,
    cell,
    motion,
    warmth,
    mass,
    weight,
    table,
    deposit,
    code_v,
    code_s,
    seen,
    gathered,
    sems,
):
    slots = 2 * owners
    copies = [
        pltpu.make_async_copy(a, b, sems.at[i])
        for i, (a, b) in enumerate(
            (
                (cell_hbm, cell.at[pl.ds(0, blocks)]),
                (motion_hbm, motion.at[:, pl.ds(0, blocks)]),
                (warmth_hbm, warmth.at[pl.ds(0, blocks)]),
                (mass_hbm, mass.at[pl.ds(0, blocks)]),
                (weight_hbm, weight.at[pl.ds(0, blocks)]),
            )
        )
    ]
    for copy in copies:
        copy.start()

    before = jnp.zeros((8, LANES), jnp.float32)
    total = jnp.zeros((8, LANES), jnp.float32)
    counts = []
    for t in range(owners):
        flags = recv_ref[t, 32:48].astype(jnp.float32)
        counts.append(jnp.broadcast_to(flags[8:9], (8, LANES)))
        before = before + jnp.broadcast_to(flags[9:10], (8, LANES))
        total = total + jnp.broadcast_to(flags[10:11], (8, LANES))
    divisor = jnp.maximum(total, 1.0)
    pick = pick_ref[...].astype(jnp.float32)
    quotient = (pick / divisor).astype(jnp.int32)
    divisor_int = divisor.astype(jnp.int32)
    picked = pick_ref[...] - quotient * divisor_int
    picked = jnp.where(picked < 0, picked + divisor_int, picked)
    picked = jnp.where(picked >= divisor_int, picked - divisor_int, picked)
    place = picked.astype(jnp.float32) - before
    running = jnp.zeros((8, LANES), jnp.float32)
    passed = jnp.zeros((8, LANES), jnp.float32)
    slot = jnp.zeros((8, LANES), jnp.float32)
    for t in range(owners):
        running = running + counts[t]
        beyond = running <= place
        slot = jnp.where(beyond, slot + 2.0, slot)
        passed = jnp.where(beyond, running, passed)
    slot = (slot + (place - passed)).astype(jnp.int32)
    block = (
        lax.broadcasted_iota(jnp.int32, (8, LANES), 0) * LANES
        + lax.broadcasted_iota(jnp.int32, (8, LANES), 1)
    )
    mine = (place >= 0.0) & (place < running) & (block < live_ref[0])
    code_v[...] = ordered_by_slot(jnp.where(mine, slot, -1), slots)
    to_scalar = pltpu.make_async_copy(code_v, code_s, sems.at[5])
    to_scalar.start()
    cell[blocks : blocks + 8] = jnp.zeros((8, LANES), jnp.int32)
    for k in range(3):
        motion[k, blocks : blocks + 8] = jnp.zeros((8, LANES), jnp.float32)
    warmth[blocks : blocks + 8] = jnp.zeros((8, LANES), jnp.float32)
    mass[blocks : blocks + 8] = jnp.ones((8, LANES), jnp.float32)
    weight[blocks : blocks + 8] = jnp.zeros((8, LANES), jnp.float32)

    spread = slot_relayout()
    for t in range(owners):
        rows = jnp.dot(spread, recv_ref[t], preferred_element_type=jnp.float32)
        table[8 * t : 8 * t + 8] = rows.reshape(8, 8, LANES)
    table[4 * slots : 4 * slots + 4] = jnp.zeros((4, 8, LANES), jnp.float32)

    def clear(t, carry):
        deposit[pl.ds(8 * t, 8)] = jnp.zeros((8, 8, LANES), jnp.float32)
        return carry

    lax.fori_loop(0, owners, clear, 0)
    deposit[4 * slots : 4 * slots + 4] = jnp.zeros((4, 8, LANES), jnp.float32)
    to_scalar.wait()

    found = code_s[15, 0]
    for copy in copies:
        copy.wait()

    sub = lax.broadcasted_iota(jnp.int32, (8, LANES), 0)

    def entry(n0, i):
        code = code_s[n0 >> 7, (n0 & (LANES - 1)) + i]
        return code & (ENTRY - 1), code >> ENTRY_BITS

    def look_up(j, carry):
        n0 = UA * j
        for i in range(0, UA, 2):
            slot = entry(n0, i)[1]
            tile = [table[4 * slot + k] for k in range(ROWS_Y)]
            for h in range(2):
                n = n0 + i + h
                b = entry(n0, i + h)[0]
                around = jnp.broadcast_to(cell[pl.ds(b, 1), :], (8, LANES))
                z, y = around & (LANES - 1), around >> 7
                rows = [jnp.take_along_axis(tile[k], z, axis=1) for k in range(ROWS_Y)]
                seen[n] = jnp.where(
                    y == 0, rows[0], jnp.where(y == 1, rows[1], jnp.where(y == 2, rows[2], rows[3]))
                )
        for i in range(UA):
            n = n0 + i
            b = entry(n0, i)[0]
            for k in range(3):
                gathered[k, pl.ds(n, 1), :] = motion[k, pl.ds(b, 1), :]
            gathered[3, pl.ds(n, 1), :] = warmth[pl.ds(b, 1), :]
            gathered[4, pl.ds(n, 1), :] = mass[pl.ds(b, 1), :]
            gathered[5, pl.ds(n, 1), :] = weight[pl.ds(b, 1), :]
        return carry

    lax.fori_loop(0, (found + UA - 1) // UA, look_up, 0)

    def move(j, carry):
        at = pl.multiple_of(UB * j, UB)
        rows = pl.ds(at, UB)
        gas = [seen[rows, f, :] for f in range(NF)]
        sources = coupling(
            gas,
            [gathered[k, rows, :] for k in range(3)],
            gathered[3, rows, :],
            gathered[4, rows, :],
            gathered[5, rows, :],
        )
        for f in range(NF):
            seen[rows, f, :] = sources[f]
        return carry

    lax.fori_loop(0, (found + UB - 1) // UB, move, 0)

    cell_row = lax.broadcasted_iota(jnp.int32, (LANES, LANES), 0)

    def scatter(j, carry):
        n0 = UC * j
        for i in range(0, UC, 2):
            slot = entry(n0, i)[1]
            parts, hots = [], []
            for h in range(2):
                n = n0 + i + h
                b = entry(n0, i + h)[0]
                cells = cell[pl.ds(b, 1), :]
                y = jnp.broadcast_to(cells, (8, LANES)) >> 7
                part = seen[n]
                parts.append(
                    jnp.concatenate(
                        [jnp.where(y == k, part, 0.0) for k in range(ROWS_Y)], axis=0
                    ).astype(jnp.bfloat16)
                )
                hots.append(
                    jnp.where(cell_row == (cells & (LANES - 1)), 1.0, 0.0).astype(jnp.bfloat16)
                )
            added = lax.dot_general(
                jnp.concatenate(parts, axis=1),
                jnp.concatenate(hots, axis=1),
                NT,
                preferred_element_type=jnp.float32,
            ).reshape(4, 8, LANES)
            deposit[pl.ds(4 * slot, 4)] = deposit[pl.ds(4 * slot, 4)] + added
        return carry

    lax.fori_loop(0, (found + UC - 1) // UC, scatter, 0)

    back = slot_relayout_back()
    for t in range(owners):
        rows = deposit[8 * t : 8 * t + 8].reshape(64, LANES).astype(jnp.bfloat16)
        out_ref[t] = jnp.dot(back, rows, preferred_element_type=jnp.float32).astype(jnp.bfloat16)


def diffuse_kernel(planes, flow_ref, nu_ref, xlo_ref, xhi_ref, ylo_ref, yhi_ref, out_ref):
    lane = lax.broadcasted_iota(jnp.int32, (ROWS_Y, LANES), 1)
    for f in range(NF):
        for x in range(planes):
            here = flow_ref[f, x]
            left = xlo_ref[f] if x == 0 else flow_ref[f, x - 1]
            right = xhi_ref[f] if x == planes - 1 else flow_ref[f, x + 1]
            first = ylo_ref[f, x : x + 1]
            last = yhi_ref[f, x : x + 1]
            lower = jnp.concatenate([first, here[: ROWS_Y - 1]], axis=0)
            upper = jnp.concatenate([here[1:], last], axis=0)
            back = jnp.where(lane == 0, 0.0, pltpu.roll(here, 1, 1))
            ahead = jnp.where(lane == LANES - 1, 0.0, pltpu.roll(here, LANES - 1, 1))
            laplace = right + left + upper + lower + ahead + back - 6.0 * here
            out_ref[f, x] = here + 0.5 * nu_ref[x] * laplace


def finish_kernel(planes, owners, holder_ref, adv_ref, recv_ref, out_ref, count):
    g = lax.axis_index("grp")
    keep = g < lax.axis_size("grp") - 1

    def clear(p, carry):
        count[p] = 0
        return carry

    lax.fori_loop(0, owners, clear, 0, unroll=True)
    for x in range(planes):
        owner = holder_ref[x]
        rank = count[owner]
        count[owner] = rank + 1
        pair = recv_ref[owner].astype(jnp.float32)
        landed = jnp.where(rank == 0, pair[:HALF], pair[HALF : 2 * HALF])
        for f in range(NF):
            value = adv_ref[f, x] + landed[ROWS_Y * f : ROWS_Y * f + ROWS_Y]
            out_ref[f, x] = jnp.where(keep, value, 0.0)


def couple_call(live, pick, arrived, cell, motion, warmth, mass, weight):
    owners, blocks = arrived.shape[0], cell.shape[0]
    vmem = pl.BlockSpec(memory_space=pltpu.VMEM)
    smem = pl.BlockSpec(memory_space=pltpu.SMEM)
    hbm = pl.BlockSpec(memory_space=pl.ANY)
    params = pltpu.CompilerParams(vmem_limit_bytes=COUPLE_VMEM)
    message = jax.ShapeDtypeStruct((owners, PAIR, LANES), jnp.bfloat16)

    def couple_body(*refs):
        couple_kernel(owners, blocks, *refs)

    return pl.pallas_call(
        couple_body,
        out_shape=message,
        in_specs=[smem, vmem, vmem] + [hbm] * 5,
        out_specs=vmem,
        scratch_shapes=[
            pltpu.VMEM((blocks + 8, LANES), jnp.int32),
            pltpu.VMEM((3, blocks + 8, LANES), jnp.float32),
            pltpu.VMEM((blocks + 8, LANES), jnp.float32),
            pltpu.VMEM((blocks + 8, LANES), jnp.float32),
            pltpu.VMEM((blocks + 8, LANES), jnp.float32),
            pltpu.VMEM((8 * owners + 4, 8, LANES), jnp.float32),
            pltpu.VMEM((8 * owners + 4, 8, LANES), jnp.float32),
            pltpu.VMEM((16, LANES), jnp.int32),
            pltpu.SMEM((16, LANES), jnp.int32),
            pltpu.VMEM((blocks + 96, 8, LANES), jnp.float32),
            pltpu.VMEM((6, blocks + 96, LANES), jnp.float32),
            pltpu.SemaphoreType.DMA((6,)),
        ],
        compiler_params=params,
    )(live, pick, arrived, cell, motion.transpose(1, 0, 2), warmth, mass, weight)


def local(
    flow_fields,
    turbulent_diffusivity,
    holder_unit,
    spray_volume_position,
    patch_pick_unreduced,
    droplet_motion,
    droplet_warmth,
    droplet_weightiness,
    droplet_multiplicity,
    living_spray_batches,
):
    groups = lax.axis_size("grp")
    owners = lax.axis_size("tile")
    planes = flow_fields.shape[1]
    blocks = spray_volume_position.shape[1]
    vmem = pl.BlockSpec(memory_space=pltpu.VMEM)
    smem = pl.BlockSpec(memory_space=pltpu.SMEM)
    params = pltpu.CompilerParams(vmem_limit_bytes=VMEM_LIMIT)

    holder = holder_unit.reshape(planes)
    own_row = holder[None]

    gas = groups - 1
    round_up = [(i, (i + 1) % gas) for i in range(gas)]
    up = lax.ppermute(own_row, "grp", round_up)
    down = lax.ppermute(own_row, "grp", [(b, a) for a, b in round_up])

    def pack_body(*refs):
        pack_kernel(planes, owners, *refs)

    packed = pl.pallas_call(
        pack_body,
        out_shape=jax.ShapeDtypeStruct((owners, PAIR, LANES), jnp.bfloat16),
        in_specs=[smem] + [vmem] * 4,
        out_specs=vmem,
        scratch_shapes=[pltpu.SMEM((2 * owners,), jnp.int32), pltpu.SMEM((owners,), jnp.int32)],
        compiler_params=params,
    )(holder, own_row, up, down, flow_fields)

    packed, top, bottom = lax.optimization_barrier(
        (packed, flow_fields[:, :, ROWS_Y - 1], flow_fields[:, :, 0])
    )
    arrived = lax.all_to_all(packed, "tile", 0, 0, tiled=True)
    up_grp = [(i, i + 1) for i in range(gas - 1)]
    ylo = lax.ppermute(top, "grp", up_grp)
    yhi = lax.ppermute(bottom, "grp", [(b, a) for a, b in up_grp])
    arrived, ylo, yhi = lax.optimization_barrier((arrived, ylo, yhi))
    outgoing = couple_call(
        living_spray_batches,
        patch_pick_unreduced.reshape(8, LANES),
        arrived,
        spray_volume_position[0],
        droplet_motion[0],
        droplet_warmth[0],
        droplet_weightiness[0],
        droplet_multiplicity[0],
    )

    outgoing, back_plane, front_plane = lax.optimization_barrier(
        (outgoing, flow_fields[:, planes - 1], flow_fields[:, 0])
    )
    landed = lax.all_to_all(outgoing, "tile", 0, 0, tiled=True)
    up_tile = [(i, i + 1) for i in range(owners - 1)]
    xlo = lax.ppermute(back_plane, "tile", up_tile)
    xhi = lax.ppermute(front_plane, "tile", [(b, a) for a, b in up_tile])

    def diffuse_body(*refs):
        diffuse_kernel(planes, *refs)

    diffused = pl.pallas_call(
        diffuse_body,
        out_shape=jax.ShapeDtypeStruct(flow_fields.shape, jnp.float32),
        in_specs=[vmem] * 6,
        out_specs=vmem,
        compiler_params=params,
    )(flow_fields, turbulent_diffusivity, xlo, xhi, ylo, yhi)
    landed, diffused = lax.optimization_barrier((landed, diffused))
    def finish_body(*refs):
        finish_kernel(planes, owners, *refs)

    return pl.pallas_call(
        finish_body,
        out_shape=jax.ShapeDtypeStruct(flow_fields.shape, jnp.float32),
        in_specs=[smem, vmem, vmem],
        out_specs=vmem,
        scratch_shapes=[pltpu.SMEM((owners,), jnp.int32)],
        compiler_params=params,
    )(holder, diffused, landed)


def solution(mesh):
    in_specs = (
        P(None, "tile", "grp", None),
        P("tile", "grp", None),
        P("grp", "tile", None),
        P("tile", None, None),
        P("tile", None),
        P("tile", None, None, None),
        P("tile", None, None),
        P("tile", None, None),
        P("tile", None, None),
        P("tile"),
    )
    out_specs = P(None, "tile", "grp", None)
    return jax.shard_map(local, mesh=mesh, in_specs=in_specs, out_specs=out_specs, check_vma=False)
```

```python
import jax
import jax.numpy as jnp
from jax import lax
from jax.experimental import pallas as pl
from jax.experimental.pallas import tpu as pltpu
from jax.sharding import PartitionSpec as P

NF = 5
ROWS_Y = 4
LANES = 128
HALF = NF * ROWS_Y
PAIR = 48
FLAGS = 40
TAIL = 32
VMEM_LIMIT = 65400 * 1024
NT = (((1,), (1,)), ((), ()))


def pack_kernel(
    planes,
    owners,
    holder_ref,
    flow_ref,
    out_ref,
    top_ref,
    bottom_ref,
    front_ref,
    back_ref,
    plane_of,
    count,
):
    is_gas = lax.axis_index("grp") < lax.axis_size("grp") - 1

    def clear(p, carry):
        count[p] = 0
        plane_of[2 * p] = 0
        plane_of[2 * p + 1] = 0
        return carry

    lax.fori_loop(0, owners, clear, 0, unroll=True)

    def place(x, carry):
        owner = holder_ref[x]
        rank = count[owner]
        plane_of[2 * owner + jnp.minimum(rank, 1)] = x
        count[owner] = rank + 1
        return carry

    lax.fori_loop(0, planes, place, 0, unroll=True)

    for p in range(owners):
        pieces = []
        for s in range(2):
            x = plane_of[2 * p + s]
            pieces += [flow_ref[f, x] for f in range(NF)]
        number = jnp.where(is_gas, count[p], 0).astype(jnp.float32)
        pieces.append(jnp.full((PAIR - FLAGS, LANES), number))
        out_ref[p] = jnp.concatenate(pieces, axis=0).astype(jnp.bfloat16)

    for f in range(NF):
        for x in range(planes):
            r = f * planes + x
            top_ref[r : r + 1] = flow_ref[f, x, ROWS_Y - 1 :]
            bottom_ref[r : r + 1] = flow_ref[f, x, :1]
        front_ref[f] = flow_ref[f, 0]
        back_ref[f] = flow_ref[f, planes - 1]


def slot_relayout():
    r = lax.broadcasted_iota(jnp.int32, (64, PAIR), 0)
    c = lax.broadcasted_iota(jnp.int32, (64, PAIR), 1)
    f = r & 7
    want = (r >> 5) * HALF + f * ROWS_Y + ((r >> 3) & 3)
    return jnp.where((f < NF) & (c == want), 1.0, 0.0).astype(jnp.bfloat16)


def slot_relayout_back():
    r = lax.broadcasted_iota(jnp.int32, (PAIR, 64), 0)
    c = lax.broadcasted_iota(jnp.int32, (PAIR, 64), 1)
    f = c & 7
    want = (c >> 5) * HALF + f * ROWS_Y + ((c >> 3) & 3)
    return jnp.where((f < NF) & (r == want), 1.0, 0.0).astype(jnp.bfloat16)


def coupling(gas, motion, warmth, mass, weight):
    relative = [gas[k] - motion[k] for k in range(3)]
    speed_sq = relative[0] * relative[0] + relative[1] * relative[1] + relative[2] * relative[2]
    inv_surface = jnp.exp((-2.0 / 3.0) * jnp.log(mass))
    drag = 0.8 * (1.0 + 0.15 * jnp.exp(0.3435 * jnp.log(1.0 + speed_sq)))
    inverse_tau = drag * inv_surface
    relaxation = 1.0 - jnp.exp(-0.5 * inverse_tau)
    heating = 1.0 / (1.0 + jnp.exp(gas[4] - gas[3]))
    remain = jnp.exp(-0.3 * heating * inv_surface)
    new_mass = mass * remain
    warming = 1.0 - jnp.exp(-0.25 * inverse_tau)
    new_warmth = warmth + warming * (gas[3] - warmth) - 0.5 * (1.0 - remain)
    out = []
    for k in range(3):
        new_velocity = motion[k] + relaxation * relative[k]
        out.append(weight * (mass * motion[k] - new_mass * new_velocity))
    out.append(weight * (mass * warmth - new_mass * new_warmth))
    out.append(weight * (mass - new_mass))
    return out


UA, UB, UC = 32, 32, 32
ENTRY_BITS = 11
ENTRY = 1 << ENTRY_BITS


def ordered_by_slot(slot, slots):
    lanes = slot.shape[1]
    spare = slots * ENTRY + slot.shape[0] * lanes
    slot_row = lax.broadcasted_iota(jnp.int32, (slots, lanes), 0)
    hits = [slot_row == jnp.broadcast_to(slot[r : r + 1], (slots, lanes)) for r in range(8)]
    p = lax.broadcasted_iota(jnp.int32, (lanes, 2 * lanes), 0)
    q = lax.broadcasted_iota(jnp.int32, (lanes, 2 * lanes), 1)
    upto = jnp.where(p <= q, 1.0, 0.0).astype(jnp.bfloat16)
    ones = jnp.concatenate([jnp.where(h, 1.0, 0.0).astype(jnp.bfloat16) for h in hits], axis=0)
    tally = jnp.dot(ones, upto, preferred_element_type=jnp.float32)
    count = sum(tally[slots * r : slots * (r + 1), lanes:] for r in range(8))
    pairs = ((count.astype(jnp.int32) + 1) >> 1)
    p = lax.broadcasted_iota(jnp.int32, (slots, slots), 0)
    q = lax.broadcasted_iota(jnp.int32, (slots, slots), 1)
    before = jnp.where(q < p, 1.0, 0.0).astype(jnp.bfloat16)
    halves = jnp.concatenate([(pairs >> 4).astype(jnp.float32), (pairs & 15).astype(jnp.float32)], axis=1)
    ahead = jnp.dot(before, halves.astype(jnp.bfloat16), preferred_element_type=jnp.float32)
    start = 2.0 * (16.0 * ahead[:, :lanes] + ahead[:, lanes:])
    number = start[slots - 1 :].astype(jnp.int32) + 2 * pairs[slots - 1 :]
    carry = start - 1.0
    low = lax.broadcasted_iota(jnp.int32, (lanes, lanes), 0)
    high = lax.broadcasted_iota(jnp.int32, (16, lanes), 0)
    lane = lax.broadcasted_iota(jnp.int32, (16, lanes), 1).astype(jnp.float32)
    values, places = [], []
    for r in range(8):
        here = tally[slots * r : slots * (r + 1)]
        at = jnp.sum(jnp.where(hits[r], here[:, :lanes] + carry, 0.0), axis=0, keepdims=True)
        carry = carry + here[:, lanes:]
        own = slot[r : r + 1]
        at = jnp.where(own >= 0, at.astype(jnp.int32), -1)
        mask = high == (at >> 7)
        for_own = jnp.broadcast_to(own.astype(jnp.float32), (16, lanes))
        values.append(
            jnp.concatenate(
                [jnp.where(mask, v, 0.0) for v in (1.0, float(r), lane, for_own)], axis=0
            ).astype(jnp.bfloat16)
        )
        places.append(jnp.where(low == (at & (lanes - 1)), 1.0, 0.0).astype(jnp.bfloat16))
    found = lax.dot_general(
        jnp.concatenate(values, axis=1),
        jnp.concatenate(places, axis=1),
        NT,
        preferred_element_type=jnp.float32,
    )
    code = found[48:64] * float(ENTRY) + found[16:32] * float(lanes) + found[32:48]
    code = jnp.where(found[:16] > 0.5, code.astype(jnp.int32), spare)
    return jnp.where(high == 15, jnp.broadcast_to(number, (16, lanes)), code)


def couple_kernel(
    owners,
    blocks,
    live_ref,
    pick_ref,
    recv_ref,
    above_ref,
    below_ref,
    far_ref,
    cell_hbm,
    motion_hbm,
    warmth_hbm,
    mass_hbm,
    weight_hbm,
    out_ref,
    cell,
    motion,
    warmth,
    mass,
    weight,
    table,
    deposit,
    code_v,
    code_s,
    seen,
    gathered,
    sems,
):
    slots = 2 * owners
    copies = [
        pltpu.make_async_copy(a, b, sems.at[i])
        for i, (a, b) in enumerate(
            (
                (cell_hbm, cell.at[pl.ds(0, blocks)]),
                (motion_hbm, motion.at[:, pl.ds(0, blocks)]),
                (warmth_hbm, warmth.at[pl.ds(0, blocks)]),
                (mass_hbm, mass.at[pl.ds(0, blocks)]),
                (weight_hbm, weight.at[pl.ds(0, blocks)]),
            )
        )
    ]
    for copy in copies:
        copy.start()

    g = lax.axis_index("grp")
    counts = []
    for t in range(owners):
        flags = recv_ref[t, TAIL:].astype(jnp.float32)[FLAGS - TAIL :]
        counts.append(jnp.broadcast_to(flags[0:1], (8, LANES)))
    gas_groups = lax.axis_size("grp") - 1
    near_above = jnp.where(g >= 1, above_ref[...], 0.0)
    near_below = jnp.where(g < gas_groups - 1, below_ref[...], 0.0)
    far = jnp.where((g + 2) % lax.axis_size("grp") < gas_groups, far_ref[...], 0.0)
    total = sum(counts) + near_above + near_below + far
    before = near_above + jnp.where(g == gas_groups - 1, far, 0.0)
    divisor = jnp.maximum(total, 1.0)
    pick = pick_ref[...].astype(jnp.float32)
    quotient = (pick / divisor).astype(jnp.int32)
    divisor_int = divisor.astype(jnp.int32)
    picked = pick_ref[...] - quotient * divisor_int
    picked = jnp.where(picked < 0, picked + divisor_int, picked)
    picked = jnp.where(picked >= divisor_int, picked - divisor_int, picked)
    place = picked.astype(jnp.float32) - before
    running = jnp.zeros((8, LANES), jnp.float32)
    passed = jnp.zeros((8, LANES), jnp.float32)
    slot = jnp.zeros((8, LANES), jnp.float32)
    for t in range(owners):
        running = running + counts[t]
        beyond = running <= place
        slot = jnp.where(beyond, slot + 2.0, slot)
        passed = jnp.where(beyond, running, passed)
    slot = (slot + (place - passed)).astype(jnp.int32)
    block = (
        lax.broadcasted_iota(jnp.int32, (8, LANES), 0) * LANES
        + lax.broadcasted_iota(jnp.int32, (8, LANES), 1)
    )
    mine = (place >= 0.0) & (place < running) & (block < live_ref[0])
    code_v[...] = ordered_by_slot(jnp.where(mine, slot, -1), slots)
    to_scalar = pltpu.make_async_copy(code_v, code_s, sems.at[5])
    to_scalar.start()
    cell[blocks : blocks + 8] = jnp.zeros((8, LANES), jnp.int32)
    for k in range(3):
        motion[k, blocks : blocks + 8] = jnp.zeros((8, LANES), jnp.float32)
    warmth[blocks : blocks + 8] = jnp.zeros((8, LANES), jnp.float32)
    mass[blocks : blocks + 8] = jnp.ones((8, LANES), jnp.float32)
    weight[blocks : blocks + 8] = jnp.zeros((8, LANES), jnp.float32)

    spread = slot_relayout()
    for t in range(owners):
        rows = jnp.dot(spread, recv_ref[t], preferred_element_type=jnp.float32)
        table[8 * t : 8 * t + 8] = rows.reshape(8, 8, LANES)
    table[4 * slots : 4 * slots + 4] = jnp.zeros((4, 8, LANES), jnp.float32)

    def clear(t, carry):
        deposit[pl.ds(8 * t, 8)] = jnp.zeros((8, 8, LANES), jnp.float32)
        return carry

    lax.fori_loop(0, owners, clear, 0)
    deposit[4 * slots : 4 * slots + 4] = jnp.zeros((4, 8, LANES), jnp.float32)
    to_scalar.wait()

    found = code_s[15, 0]
    for copy in copies:
        copy.wait()

    sub = lax.broadcasted_iota(jnp.int32, (8, LANES), 0)

    def entry(n0, i):
        code = code_s[n0 >> 7, (n0 & (LANES - 1)) + i]
        return code & (ENTRY - 1), code >> ENTRY_BITS

    def look_up(j, carry):
        n0 = UA * j
        for i in range(0, UA, 2):
            slot = entry(n0, i)[1]
            tile = [table[4 * slot + k] for k in range(ROWS_Y)]
            for h in range(2):
                n = n0 + i + h
                b = entry(n0, i + h)[0]
                around = jnp.broadcast_to(cell[pl.ds(b, 1), :], (8, LANES))
                z, y = around & (LANES - 1), around >> 7
                rows = [jnp.take_along_axis(tile[k], z, axis=1) for k in range(ROWS_Y)]
                seen[n] = jnp.where(
                    y == 0, rows[0], jnp.where(y == 1, rows[1], jnp.where(y == 2, rows[2], rows[3]))
                )
        for i in range(UA):
            n = n0 + i
            b = entry(n0, i)[0]
            for k in range(3):
                gathered[k, pl.ds(n, 1), :] = motion[k, pl.ds(b, 1), :]
            gathered[3, pl.ds(n, 1), :] = warmth[pl.ds(b, 1), :]
            gathered[4, pl.ds(n, 1), :] = mass[pl.ds(b, 1), :]
            gathered[5, pl.ds(n, 1), :] = weight[pl.ds(b, 1), :]
        return carry

    lax.fori_loop(0, (found + UA - 1) // UA, look_up, 0)

    def move(j, carry):
        at = pl.multiple_of(UB * j, UB)
        rows = pl.ds(at, UB)
        gas = [seen[rows, f, :] for f in range(NF)]
        sources = coupling(
            gas,
            [gathered[k, rows, :] for k in range(3)],
            gathered[3, rows, :],
            gathered[4, rows, :],
            gathered[5, rows, :],
        )
        for f in range(NF):
            seen[rows, f, :] = sources[f]
        return carry

    lax.fori_loop(0, (found + UB - 1) // UB, move, 0)

    cell_row = lax.broadcasted_iota(jnp.int32, (LANES, LANES), 0)

    def scatter(j, carry):
        n0 = UC * j
        for i in range(0, UC, 2):
            slot = entry(n0, i)[1]
            parts, hots = [], []
            for h in range(2):
                n = n0 + i + h
                b = entry(n0, i + h)[0]
                cells = cell[pl.ds(b, 1), :]
                y = jnp.broadcast_to(cells, (8, LANES)) >> 7
                part = seen[n]
                parts.append(
                    jnp.concatenate(
                        [jnp.where(y == k, part, 0.0) for k in range(ROWS_Y)], axis=0
                    ).astype(jnp.bfloat16)
                )
                hots.append(
                    jnp.where(cell_row == (cells & (LANES - 1)), 1.0, 0.0).astype(jnp.bfloat16)
                )
            added = lax.dot_general(
                jnp.concatenate(parts, axis=1),
                jnp.concatenate(hots, axis=1),
                NT,
                preferred_element_type=jnp.float32,
            ).reshape(4, 8, LANES)
            deposit[pl.ds(4 * slot, 4)] = deposit[pl.ds(4 * slot, 4)] + added
        return carry

    lax.fori_loop(0, (found + UC - 1) // UC, scatter, 0)

    back = slot_relayout_back()
    for t in range(owners):
        rows = deposit[8 * t : 8 * t + 8].reshape(64, LANES).astype(jnp.bfloat16)
        out_ref[t] = jnp.dot(back, rows, preferred_element_type=jnp.float32).astype(jnp.bfloat16)


def finish_kernel(
    planes,
    owners,
    holder_ref,
    flow_ref,
    nu_ref,
    xlo_ref,
    xhi_ref,
    up_ref,
    down_ref,
    landed_ref,
    out_ref,
    count,
):
    me = lax.axis_index("tile")
    g = lax.axis_index("grp")
    gas_groups = lax.axis_size("grp") - 1
    lane = lax.broadcasted_iota(jnp.int32, (ROWS_Y, LANES), 1)

    def clear(p, carry):
        count[p] = 0
        return carry

    lax.fori_loop(0, owners, clear, 0, unroll=True)

    xlo = [jnp.where(me > 0, xlo_ref[f], 0.0) for f in range(NF)]
    xhi = [jnp.where(me < owners - 1, xhi_ref[f], 0.0) for f in range(NF)]
    for x in range(planes):
        owner = holder_ref[x]
        rank = count[owner]
        count[owner] = rank + 1
        pair = landed_ref[owner].astype(jnp.float32)
        landed = jnp.where(rank == 0, pair[:HALF], pair[HALF : 2 * HALF])
        for f in range(NF):
            r = f * planes + x
            here = flow_ref[f, x]
            left = xlo[f] if x == 0 else flow_ref[f, x - 1]
            right = xhi[f] if x == planes - 1 else flow_ref[f, x + 1]
            first = jnp.where(g >= 1, up_ref[r : r + 1], 0.0)
            last = jnp.where(g < gas_groups - 1, down_ref[r : r + 1], 0.0)
            lower = jnp.concatenate([first, here[: ROWS_Y - 1]], axis=0)
            upper = jnp.concatenate([here[1:], last], axis=0)
            back = jnp.where(lane == 0, 0.0, pltpu.roll(here, 1, 1))
            ahead = jnp.where(lane == LANES - 1, 0.0, pltpu.roll(here, LANES - 1, 1))
            laplace = right + left + upper + lower + ahead + back - 6.0 * here
            value = here + 0.5 * nu_ref[x] * laplace + landed[ROWS_Y * f : ROWS_Y * f + ROWS_Y]
            out_ref[f, x] = jnp.where(g < gas_groups, value, 0.0)


def couple_call(live, pick, arrived, above, below, far, cell, motion, warmth, mass, weight):
    owners, blocks = arrived.shape[0], cell.shape[0]
    vmem = pl.BlockSpec(memory_space=pltpu.VMEM)
    smem = pl.BlockSpec(memory_space=pltpu.SMEM)
    hbm = pl.BlockSpec(memory_space=pl.ANY)
    params = pltpu.CompilerParams(vmem_limit_bytes=VMEM_LIMIT)
    message = jax.ShapeDtypeStruct((owners, PAIR, LANES), jnp.bfloat16)

    def couple_body(*refs):
        couple_kernel(owners, blocks, *refs)

    return pl.pallas_call(
        couple_body,
        out_shape=message,
        in_specs=[smem] + [vmem] * 5 + [hbm] * 5,
        out_specs=vmem,
        scratch_shapes=[
            pltpu.VMEM((blocks + 8, LANES), jnp.int32),
            pltpu.VMEM((3, blocks + 8, LANES), jnp.float32),
            pltpu.VMEM((blocks + 8, LANES), jnp.float32),
            pltpu.VMEM((blocks + 8, LANES), jnp.float32),
            pltpu.VMEM((blocks + 8, LANES), jnp.float32),
            pltpu.VMEM((8 * owners + 4, 8, LANES), jnp.float32),
            pltpu.VMEM((8 * owners + 4, 8, LANES), jnp.float32),
            pltpu.VMEM((16, LANES), jnp.int32),
            pltpu.SMEM((16, LANES), jnp.int32),
            pltpu.VMEM((blocks + 96, 8, LANES), jnp.float32),
            pltpu.VMEM((6, blocks + 96, LANES), jnp.float32),
            pltpu.SemaphoreType.DMA((6,)),
        ],
        compiler_params=params,
    )(live, pick, arrived, above, below, far, cell, motion.transpose(1, 0, 2), warmth, mass, weight)


def local(
    flow_fields,
    turbulent_diffusivity,
    holder_unit,
    spray_volume_position,
    patch_pick_unreduced,
    droplet_motion,
    droplet_warmth,
    droplet_weightiness,
    droplet_multiplicity,
    living_spray_batches,
):
    groups = lax.axis_size("grp")
    owners = lax.axis_size("tile")
    planes = flow_fields.shape[1]
    blocks = spray_volume_position.shape[1]
    vmem = pl.BlockSpec(memory_space=pltpu.VMEM)
    smem = pl.BlockSpec(memory_space=pltpu.SMEM)
    params = pltpu.CompilerParams(vmem_limit_bytes=VMEM_LIMIT)

    holder = holder_unit.reshape(planes)

    def pack_body(*refs):
        pack_kernel(planes, owners, *refs)

    edge = jax.ShapeDtypeStruct((NF * planes, LANES), jnp.float32)
    plane = jax.ShapeDtypeStruct((NF, ROWS_Y, LANES), jnp.float32)
    packed, top, bottom, front, behind = pl.pallas_call(
        pack_body,
        out_shape=(
            jax.ShapeDtypeStruct((owners, PAIR, LANES), jnp.bfloat16),
            edge,
            edge,
            plane,
            plane,
        ),
        in_specs=[smem, vmem],
        out_specs=(vmem,) * 5,
        scratch_shapes=[pltpu.SMEM((2 * owners,), jnp.int32), pltpu.SMEM((owners,), jnp.int32)],
        compiler_params=params,
    )(holder, flow_fields)

    def turned(array, axis, step):
        size = lax.axis_size(axis)
        return lax.ppermute(array, axis, [(i, (i + step) % size) for i in range(size)])

    arrived = lax.all_to_all(packed, "tile", 0, 0, tiled=True)
    xlo = turned(behind, "tile", 1)
    xhi = turned(front, "tile", owners - 1)
    arrived, xlo, xhi = lax.optimization_barrier((arrived, xlo, xhi))

    number = jnp.sum(arrived[:, FLAGS:].astype(jnp.float32), axis=0)
    above, far, below = (turned(number, "grp", k) for k in range(1, groups))

    outgoing = couple_call(
        living_spray_batches,
        patch_pick_unreduced.reshape(8, LANES),
        arrived,
        above,
        below,
        far,
        spray_volume_position[0],
        droplet_motion[0],
        droplet_warmth[0],
        droplet_weightiness[0],
        droplet_multiplicity[0],
    )

    outgoing, top, bottom = lax.optimization_barrier((outgoing, top, bottom))
    landed = lax.all_to_all(outgoing, "tile", 0, 0, tiled=True)
    up = turned(top, "grp", 1)
    down = turned(bottom, "grp", groups - 1)

    def finish_body(*refs):
        finish_kernel(planes, owners, *refs)

    return pl.pallas_call(
        finish_body,
        out_shape=jax.ShapeDtypeStruct(flow_fields.shape, jnp.float32),
        in_specs=[smem] + [vmem] * 7,
        out_specs=vmem,
        scratch_shapes=[pltpu.SMEM((owners,), jnp.int32)],
        compiler_params=params,
    )(holder, flow_fields, turbulent_diffusivity, xlo, xhi, up, down, landed)


def solution(mesh):
    in_specs = (
        P(None, "tile", "grp", None),
        P("tile", "grp", None),
        P("grp", "tile", None),
        P("tile", None, None),
        P("tile", None),
        P("tile", None, None, None),
        P("tile", None, None),
        P("tile", None, None),
        P("tile", None, None),
        P("tile"),
    )
    out_specs = P(None, "tile", "grp", None)
    return jax.shard_map(local, mesh=mesh, in_specs=in_specs, out_specs=out_specs, check_vma=False)
```

```python
import jax
import jax.numpy as jnp
from jax import lax
from jax.experimental import pallas as pl
from jax.experimental.pallas import tpu as pltpu
from jax.sharding import PartitionSpec as P

NF = 5
ROWS_Y = 4
LANES = 128
HALF = NF * ROWS_Y
PAIR = 48
FLAGS = 40
TAIL = 32
VMEM_LIMIT = 65400 * 1024
NT = (((1,), (1,)), ((), ()))


def pack_kernel(
    planes,
    owners,
    holder_ref,
    flow_ref,
    out_ref,
    top_ref,
    bottom_ref,
    front_ref,
    back_ref,
    plane_of,
    count,
):
    is_gas = lax.axis_index("grp") < lax.axis_size("grp") - 1

    def clear(p, carry):
        count[p] = 0
        plane_of[2 * p] = 0
        plane_of[2 * p + 1] = 0
        return carry

    lax.fori_loop(0, owners, clear, 0, unroll=True)

    def place(x, carry):
        owner = holder_ref[x]
        rank = count[owner]
        plane_of[2 * owner + jnp.minimum(rank, 1)] = x
        count[owner] = rank + 1
        return carry

    lax.fori_loop(0, planes, place, 0, unroll=True)

    for p in range(owners):
        pieces = []
        for s in range(2):
            x = plane_of[2 * p + s]
            pieces += [flow_ref[f, x] for f in range(NF)]
        number = jnp.where(is_gas, count[p], 0).astype(jnp.float32)
        pieces.append(jnp.full((PAIR - FLAGS, LANES), number))
        out_ref[p] = jnp.concatenate(pieces, axis=0).astype(jnp.bfloat16)

    for f in range(NF):
        for x in range(planes):
            r = f * planes + x
            top_ref[r : r + 1] = flow_ref[f, x, ROWS_Y - 1 :]
            bottom_ref[r : r + 1] = flow_ref[f, x, :1]
        front_ref[f] = flow_ref[f, 0]
        back_ref[f] = flow_ref[f, planes - 1]


def slot_relayout():
    r = lax.broadcasted_iota(jnp.int32, (64, PAIR), 0)
    c = lax.broadcasted_iota(jnp.int32, (64, PAIR), 1)
    f = r & 7
    want = (r >> 5) * HALF + f * ROWS_Y + ((r >> 3) & 3)
    return jnp.where((f < NF) & (c == want), 1.0, 0.0).astype(jnp.bfloat16)


def slot_relayout_back():
    r = lax.broadcasted_iota(jnp.int32, (PAIR, 64), 0)
    c = lax.broadcasted_iota(jnp.int32, (PAIR, 64), 1)
    f = c & 7
    want = (c >> 5) * HALF + f * ROWS_Y + ((c >> 3) & 3)
    return jnp.where((f < NF) & (r == want), 1.0, 0.0).astype(jnp.bfloat16)


def coupling(gas, motion, warmth, mass, weight):
    relative = [gas[k] - motion[k] for k in range(3)]
    speed_sq = relative[0] * relative[0] + relative[1] * relative[1] + relative[2] * relative[2]
    inv_surface = jnp.exp((-2.0 / 3.0) * jnp.log(mass))
    drag = 0.8 * (1.0 + 0.15 * jnp.exp(0.3435 * jnp.log(1.0 + speed_sq)))
    inverse_tau = drag * inv_surface
    relaxation = 1.0 - jnp.exp(-0.5 * inverse_tau)
    heating = 1.0 / (1.0 + jnp.exp(gas[4] - gas[3]))
    remain = jnp.exp(-0.3 * heating * inv_surface)
    new_mass = mass * remain
    warming = 1.0 - jnp.exp(-0.25 * inverse_tau)
    new_warmth = warmth + warming * (gas[3] - warmth) - 0.5 * (1.0 - remain)
    out = []
    for k in range(3):
        new_velocity = motion[k] + relaxation * relative[k]
        out.append(weight * (mass * motion[k] - new_mass * new_velocity))
    out.append(weight * (mass * warmth - new_mass * new_warmth))
    out.append(weight * (mass - new_mass))
    return out


STEP = 32
ENTRY_BITS = 11
ENTRY = 1 << ENTRY_BITS


def ordered_by_slot(slot, slots):
    lanes = slot.shape[1]
    spare = slots * ENTRY + slot.shape[0] * lanes
    slot_row = lax.broadcasted_iota(jnp.int32, (slots, lanes), 0)
    hits = [slot_row == jnp.broadcast_to(slot[r : r + 1], (slots, lanes)) for r in range(8)]
    p = lax.broadcasted_iota(jnp.int32, (lanes, 2 * lanes), 0)
    q = lax.broadcasted_iota(jnp.int32, (lanes, 2 * lanes), 1)
    upto = jnp.where(p <= q, 1.0, 0.0).astype(jnp.bfloat16)
    ones = jnp.concatenate([jnp.where(h, 1.0, 0.0).astype(jnp.bfloat16) for h in hits], axis=0)
    tally = jnp.dot(ones, upto, preferred_element_type=jnp.float32)
    count = sum(tally[slots * r : slots * (r + 1), lanes:] for r in range(8))
    pairs = ((count.astype(jnp.int32) + 1) >> 1)
    p = lax.broadcasted_iota(jnp.int32, (slots, slots), 0)
    q = lax.broadcasted_iota(jnp.int32, (slots, slots), 1)
    before = jnp.where(q < p, 1.0, 0.0).astype(jnp.bfloat16)
    halves = jnp.concatenate([(pairs >> 4).astype(jnp.float32), (pairs & 15).astype(jnp.float32)], axis=1)
    ahead = jnp.dot(before, halves.astype(jnp.bfloat16), preferred_element_type=jnp.float32)
    start = 2.0 * (16.0 * ahead[:, :lanes] + ahead[:, lanes:])
    number = start[slots - 1 :].astype(jnp.int32) + 2 * pairs[slots - 1 :]
    carry = start + (2 * STEP - 1.0)
    low = lax.broadcasted_iota(jnp.int32, (lanes, lanes), 0)
    high = lax.broadcasted_iota(jnp.int32, (16, lanes), 0)
    lane = lax.broadcasted_iota(jnp.int32, (16, lanes), 1).astype(jnp.float32)
    values, places = [], []
    for r in range(8):
        here = tally[slots * r : slots * (r + 1)]
        at = jnp.sum(jnp.where(hits[r], here[:, :lanes] + carry, 0.0), axis=0, keepdims=True)
        carry = carry + here[:, lanes:]
        own = slot[r : r + 1]
        at = jnp.where(own >= 0, at.astype(jnp.int32), -1)
        mask = high == (at >> 7)
        for_own = jnp.broadcast_to(own.astype(jnp.float32), (16, lanes))
        values.append(
            jnp.concatenate(
                [jnp.where(mask, v, 0.0) for v in (1.0, float(r), lane, for_own)], axis=0
            ).astype(jnp.bfloat16)
        )
        places.append(jnp.where(low == (at & (lanes - 1)), 1.0, 0.0).astype(jnp.bfloat16))
    found = lax.dot_general(
        jnp.concatenate(values, axis=1),
        jnp.concatenate(places, axis=1),
        NT,
        preferred_element_type=jnp.float32,
    )
    code = found[48:64] * float(ENTRY) + found[16:32] * float(lanes) + found[32:48]
    code = jnp.where(found[:16] > 0.5, code.astype(jnp.int32), spare)
    return jnp.where(high == 15, jnp.broadcast_to(number, (16, lanes)), code)


def couple_kernel(
    owners,
    blocks,
    live_ref,
    pick_ref,
    recv_ref,
    above_ref,
    below_ref,
    far_ref,
    cell_hbm,
    motion_hbm,
    warmth_hbm,
    mass_hbm,
    weight_hbm,
    out_ref,
    cell,
    motion,
    warmth,
    mass,
    weight,
    table,
    deposit,
    code_v,
    code_s,
    seen,
    gathered,
    source,
    sems,
):
    slots = 2 * owners
    copies = [
        pltpu.make_async_copy(a, b, sems.at[i])
        for i, (a, b) in enumerate(
            (
                (cell_hbm, cell.at[pl.ds(0, blocks)]),
                (motion_hbm, motion.at[:, pl.ds(0, blocks)]),
                (warmth_hbm, warmth.at[pl.ds(0, blocks)]),
                (mass_hbm, mass.at[pl.ds(0, blocks)]),
                (weight_hbm, weight.at[pl.ds(0, blocks)]),
            )
        )
    ]
    for copy in copies:
        copy.start()

    g = lax.axis_index("grp")
    counts = []
    for t in range(owners):
        flags = recv_ref[t, TAIL:].astype(jnp.float32)[FLAGS - TAIL :]
        counts.append(jnp.broadcast_to(flags[0:1], (8, LANES)))
    gas_groups = lax.axis_size("grp") - 1
    near_above = jnp.where(g >= 1, above_ref[...], 0.0)
    near_below = jnp.where(g < gas_groups - 1, below_ref[...], 0.0)
    far = jnp.where((g + 2) % lax.axis_size("grp") < gas_groups, far_ref[...], 0.0)
    total = sum(counts) + near_above + near_below + far
    before = near_above + jnp.where(g == gas_groups - 1, far, 0.0)
    divisor = jnp.maximum(total, 1.0)
    pick = pick_ref[...].astype(jnp.float32)
    quotient = (pick / divisor).astype(jnp.int32)
    divisor_int = divisor.astype(jnp.int32)
    picked = pick_ref[...] - quotient * divisor_int
    picked = jnp.where(picked < 0, picked + divisor_int, picked)
    picked = jnp.where(picked >= divisor_int, picked - divisor_int, picked)
    place = picked.astype(jnp.float32) - before
    running = jnp.zeros((8, LANES), jnp.float32)
    passed = jnp.zeros((8, LANES), jnp.float32)
    slot = jnp.zeros((8, LANES), jnp.float32)
    for t in range(owners):
        running = running + counts[t]
        beyond = running <= place
        slot = jnp.where(beyond, slot + 2.0, slot)
        passed = jnp.where(beyond, running, passed)
    slot = (slot + (place - passed)).astype(jnp.int32)
    block = (
        lax.broadcasted_iota(jnp.int32, (8, LANES), 0) * LANES
        + lax.broadcasted_iota(jnp.int32, (8, LANES), 1)
    )
    mine = (place >= 0.0) & (place < running) & (block < live_ref[0])
    code_v[...] = ordered_by_slot(jnp.where(mine, slot, -1), slots)
    to_scalar = pltpu.make_async_copy(code_v, code_s, sems.at[5])
    to_scalar.start()
    cell[blocks : blocks + 8] = jnp.zeros((8, LANES), jnp.int32)
    for k in range(3):
        motion[k, blocks : blocks + 8] = jnp.zeros((8, LANES), jnp.float32)
    warmth[blocks : blocks + 8] = jnp.zeros((8, LANES), jnp.float32)
    mass[blocks : blocks + 8] = jnp.ones((8, LANES), jnp.float32)
    weight[blocks : blocks + 8] = jnp.zeros((8, LANES), jnp.float32)

    spread = slot_relayout()
    for t in range(owners):
        rows = jnp.dot(spread, recv_ref[t], preferred_element_type=jnp.float32)
        table[8 * t : 8 * t + 8] = rows.reshape(8, 8, LANES)
    table[4 * slots : 4 * slots + 4] = jnp.zeros((4, 8, LANES), jnp.float32)

    def clear(t, carry):
        deposit[pl.ds(8 * t, 8)] = jnp.zeros((8, 8, LANES), jnp.float32)
        return carry

    lax.fori_loop(0, owners, clear, 0)
    deposit[4 * slots : 4 * slots + 4] = jnp.zeros((4, 8, LANES), jnp.float32)
    source[...] = jnp.zeros_like(source)
    to_scalar.wait()

    found = code_s[15, 0]
    for copy in copies:
        copy.wait()

    def entry(n0, i):
        code = code_s[n0 >> 7, (n0 & (LANES - 1)) + i]
        return code & (ENTRY - 1), code >> ENTRY_BITS

    cell_row = lax.broadcasted_iota(jnp.int32, (LANES, LANES), 0).astype(jnp.float32).astype(jnp.bfloat16)

    def look_up(j):
        n0 = STEP * j
        for i in range(0, STEP, 2):
            slot = entry(n0, i)[1]
            tile = [table[4 * slot + k] for k in range(ROWS_Y)]
            for h in range(2):
                b = entry(n0, i + h)[0]
                around = jnp.broadcast_to(cell[pl.ds(b, 1), :], (8, LANES))
                z, y = around & (LANES - 1), around >> 7
                rows = [jnp.take_along_axis(tile[k], z, axis=1) for k in range(ROWS_Y)]
                seen[i + h] = jnp.where(
                    y == 0, rows[0], jnp.where(y == 1, rows[1], jnp.where(y == 2, rows[2], rows[3]))
                )
                for k in range(3):
                    gathered[k, i + h : i + h + 1, :] = motion[k, pl.ds(b, 1), :]
                gathered[3, i + h : i + h + 1, :] = warmth[pl.ds(b, 1), :]
                gathered[4, i + h : i + h + 1, :] = mass[pl.ds(b, 1), :]
                gathered[5, i + h : i + h + 1, :] = weight[pl.ds(b, 1), :]

    def move():
        gas = [seen[:, f, :] for f in range(NF)]
        sources = coupling(
            gas,
            [gathered[k] for k in range(3)],
            gathered[3],
            gathered[4],
            gathered[5],
        )
        for f in range(NF):
            source[:, f, :] = sources[f]

    def scatter(j):
        n0 = STEP * j
        for i in range(0, STEP, 2):
            slot = entry(n0, i)[1]
            parts, hots = [], []
            for h in range(2):
                b = entry(n0, i + h)[0]
                cells = cell[pl.ds(b, 1), :]
                y = jnp.broadcast_to(cells, (8, LANES)) >> 7
                part = source[i + h]
                parts.append(
                    jnp.concatenate(
                        [jnp.where(y == k, part, 0.0) for k in range(ROWS_Y)], axis=0
                    ).astype(jnp.bfloat16)
                )
                hots.append(
                    jnp.where(cell_row == (cells & (LANES - 1)).astype(jnp.float32).astype(jnp.bfloat16), jnp.bfloat16(1), jnp.bfloat16(0))
                )
            added = lax.dot_general(
                jnp.concatenate(parts, axis=1),
                jnp.concatenate(hots, axis=1),
                NT,
                preferred_element_type=jnp.float32,
            ).reshape(4, 8, LANES)
            deposit[pl.ds(4 * slot, 4)] = deposit[pl.ds(4 * slot, 4)] + added

    def advance(j, carry):
        scatter(j)
        move()
        look_up(j + 2)
        return carry

    lax.fori_loop(0, (found + STEP - 1) // STEP + 2, advance, 0)

    back = slot_relayout_back()
    for t in range(owners):
        rows = deposit[8 * t : 8 * t + 8].reshape(64, LANES).astype(jnp.bfloat16)
        out_ref[t] = jnp.dot(back, rows, preferred_element_type=jnp.float32).astype(jnp.bfloat16)


def finish_kernel(
    planes,
    owners,
    holder_ref,
    flow_ref,
    nu_ref,
    xlo_ref,
    xhi_ref,
    up_ref,
    down_ref,
    landed_ref,
    out_ref,
    count,
):
    me = lax.axis_index("tile")
    g = lax.axis_index("grp")
    gas_groups = lax.axis_size("grp") - 1
    lane = lax.broadcasted_iota(jnp.int32, (ROWS_Y, LANES), 1)

    def clear(p, carry):
        count[p] = 0
        return carry

    lax.fori_loop(0, owners, clear, 0, unroll=True)

    xlo = [jnp.where(me > 0, xlo_ref[f], 0.0) for f in range(NF)]
    xhi = [jnp.where(me < owners - 1, xhi_ref[f], 0.0) for f in range(NF)]
    for x in range(planes):
        owner = holder_ref[x]
        rank = count[owner]
        count[owner] = rank + 1
        pair = landed_ref[owner].astype(jnp.float32)
        landed = jnp.where(rank == 0, pair[:HALF], pair[HALF : 2 * HALF])
        for f in range(NF):
            r = f * planes + x
            here = flow_ref[f, x]
            left = xlo[f] if x == 0 else flow_ref[f, x - 1]
            right = xhi[f] if x == planes - 1 else flow_ref[f, x + 1]
            first = jnp.where(g >= 1, up_ref[r : r + 1], 0.0)
            last = jnp.where(g < gas_groups - 1, down_ref[r : r + 1], 0.0)
            lower = jnp.concatenate([first, here[: ROWS_Y - 1]], axis=0)
            upper = jnp.concatenate([here[1:], last], axis=0)
            back = jnp.where(lane == 0, 0.0, pltpu.roll(here, 1, 1))
            ahead = jnp.where(lane == LANES - 1, 0.0, pltpu.roll(here, LANES - 1, 1))
            laplace = right + left + upper + lower + ahead + back - 6.0 * here
            value = here + 0.5 * nu_ref[x] * laplace + landed[ROWS_Y * f : ROWS_Y * f + ROWS_Y]
            out_ref[f, x] = jnp.where(g < gas_groups, value, 0.0)


def couple_call(live, pick, arrived, above, below, far, cell, motion, warmth, mass, weight):
    owners, blocks = arrived.shape[0], cell.shape[0]
    vmem = pl.BlockSpec(memory_space=pltpu.VMEM)
    smem = pl.BlockSpec(memory_space=pltpu.SMEM)
    hbm = pl.BlockSpec(memory_space=pl.ANY)
    params = pltpu.CompilerParams(vmem_limit_bytes=64136 * 1024)
    message = jax.ShapeDtypeStruct((owners, PAIR, LANES), jnp.bfloat16)

    def couple_body(*refs):
        couple_kernel(owners, blocks, *refs)

    return pl.pallas_call(
        couple_body,
        out_shape=message,
        in_specs=[smem] + [vmem] * 5 + [hbm] * 5,
        out_specs=vmem,
        scratch_shapes=[
            pltpu.VMEM((blocks + 8, LANES), jnp.int32),
            pltpu.VMEM((3, blocks + 8, LANES), jnp.float32),
            pltpu.VMEM((blocks + 8, LANES), jnp.float32),
            pltpu.VMEM((blocks + 8, LANES), jnp.float32),
            pltpu.VMEM((blocks + 8, LANES), jnp.float32),
            pltpu.VMEM((8 * owners + 4, 8, LANES), jnp.float32),
            pltpu.VMEM((8 * owners + 4, 8, LANES), jnp.float32),
            pltpu.VMEM((16, LANES), jnp.int32),
            pltpu.SMEM((16, LANES), jnp.int32),
            pltpu.VMEM((STEP, 8, LANES), jnp.float32),
            pltpu.VMEM((6, STEP, LANES), jnp.float32),
            pltpu.VMEM((STEP, 8, LANES), jnp.float32),
            pltpu.SemaphoreType.DMA((6,)),
        ],
        compiler_params=params,
    )(live, pick, arrived, above, below, far, cell, motion.transpose(1, 0, 2), warmth, mass, weight)


def local(
    flow_fields,
    turbulent_diffusivity,
    holder_unit,
    spray_volume_position,
    patch_pick_unreduced,
    droplet_motion,
    droplet_warmth,
    droplet_weightiness,
    droplet_multiplicity,
    living_spray_batches,
):
    groups = lax.axis_size("grp")
    owners = lax.axis_size("tile")
    planes = flow_fields.shape[1]
    blocks = spray_volume_position.shape[1]
    vmem = pl.BlockSpec(memory_space=pltpu.VMEM)
    smem = pl.BlockSpec(memory_space=pltpu.SMEM)
    params = pltpu.CompilerParams(vmem_limit_bytes=VMEM_LIMIT)

    holder = holder_unit.reshape(planes)

    def pack_body(*refs):
        pack_kernel(planes, owners, *refs)

    edge = jax.ShapeDtypeStruct((NF * planes, LANES), jnp.float32)
    plane = jax.ShapeDtypeStruct((NF, ROWS_Y, LANES), jnp.float32)
    packed, top, bottom, front, behind = pl.pallas_call(
        pack_body,
        out_shape=(
            jax.ShapeDtypeStruct((owners, PAIR, LANES), jnp.bfloat16),
            edge,
            edge,
            plane,
            plane,
        ),
        in_specs=[smem, vmem],
        out_specs=(vmem,) * 5,
        scratch_shapes=[pltpu.SMEM((2 * owners,), jnp.int32), pltpu.SMEM((owners,), jnp.int32)],
        compiler_params=params,
    )(holder, flow_fields)

    def turned(array, axis, step):
        size = lax.axis_size(axis)
        return lax.ppermute(array, axis, [(i, (i + step) % size) for i in range(size)])

    arrived = lax.all_to_all(packed, "tile", 0, 0, tiled=True)
    xlo = turned(behind, "tile", 1)
    xhi = turned(front, "tile", owners - 1)
    arrived, xlo, xhi = lax.optimization_barrier((arrived, xlo, xhi))

    number = jnp.sum(arrived[:, FLAGS:].astype(jnp.float32), axis=0)
    above, far, below = (turned(number, "grp", k) for k in range(1, groups))

    outgoing = couple_call(
        living_spray_batches,
        patch_pick_unreduced.reshape(8, LANES),
        arrived,
        above,
        below,
        far,
        spray_volume_position[0],
        droplet_motion[0],
        droplet_warmth[0],
        droplet_weightiness[0],
        droplet_multiplicity[0],
    )

    outgoing, top, bottom = lax.optimization_barrier((outgoing, top, bottom))
    landed = lax.all_to_all(outgoing, "tile", 0, 0, tiled=True)
    up = turned(top, "grp", 1)
    down = turned(bottom, "grp", groups - 1)

    def finish_body(*refs):
        finish_kernel(planes, owners, *refs)

    return pl.pallas_call(
        finish_body,
        out_shape=jax.ShapeDtypeStruct(flow_fields.shape, jnp.float32),
        in_specs=[smem] + [vmem] * 7,
        out_specs=vmem,
        scratch_shapes=[pltpu.SMEM((owners,), jnp.int32)],
        compiler_params=pltpu.CompilerParams(vmem_limit_bytes=40 * 1024 * 1024),
    )(holder, flow_fields, turbulent_diffusivity, xlo, xhi, up, down, landed)


def solution(mesh):
    in_specs = (
        P(None, "tile", "grp", None),
        P("tile", "grp", None),
        P("grp", "tile", None),
        P("tile", None, None),
        P("tile", None),
        P("tile", None, None, None),
        P("tile", None, None),
        P("tile", None, None),
        P("tile", None, None),
        P("tile"),
    )
    out_specs = P(None, "tile", "grp", None)
    return jax.shard_map(local, mesh=mesh, in_specs=in_specs, out_specs=out_specs, check_vma=False)
```

```python
import jax
import jax.numpy as jnp
from jax import lax
from jax.experimental import pallas as pl
from jax.experimental.pallas import tpu as pltpu
from jax.sharding import PartitionSpec as P

NF = 5
ROWS_Y = 4
LANES = 128
HALF = NF * ROWS_Y
PAIR = 2 * HALF
EMPTY = 2.0**100
VMEM_LIMIT = 65400 * 1024
NT = (((1,), (1,)), ((), ()))


def pack_kernel(
    planes,
    owners,
    holder_ref,
    flow_ref,
    out_ref,
    top_ref,
    bottom_ref,
    front_ref,
    back_ref,
    plane_of,
    count,
    rows_above,
    rows_below,
):
    is_gas = lax.axis_index("grp") < lax.axis_size("grp") - 1

    def clear(p, carry):
        count[p] = 0
        plane_of[2 * p] = 0
        plane_of[2 * p + 1] = 0
        return carry

    lax.fori_loop(0, owners, clear, 0, unroll=True)

    def place(x, carry):
        owner = holder_ref[x]
        rank = count[owner]
        plane_of[2 * owner + jnp.minimum(rank, 1)] = x
        count[owner] = rank + 1
        return carry

    lax.fori_loop(0, planes, place, 0, unroll=True)

    row = lax.broadcasted_iota(jnp.int32, (PAIR, LANES), 0)
    for p in range(owners):
        pieces = []
        for s in range(2):
            x = plane_of[2 * p + s]
            pieces += [flow_ref[f, x] for f in range(NF)]
        filled = HALF * jnp.where(is_gas, count[p], 0)
        rows = jnp.where(row < filled, jnp.concatenate(pieces, axis=0), EMPTY)
        out_ref[p] = rows.astype(jnp.bfloat16)

    for f in range(NF):
        for x in range(planes):
            r = f * planes + x
            rows_above[r : r + 1] = flow_ref[f, x, ROWS_Y - 1 :]
            rows_below[r : r + 1] = flow_ref[f, x, :1]
        front_ref[f] = flow_ref[f, 0]
        back_ref[f] = flow_ref[f, planes - 1]
    top_ref[...] = rows_above[...].astype(jnp.bfloat16)
    bottom_ref[...] = rows_below[...].astype(jnp.bfloat16)


def slot_relayout():
    r = lax.broadcasted_iota(jnp.int32, (64, PAIR), 0)
    c = lax.broadcasted_iota(jnp.int32, (64, PAIR), 1)
    f = r & 7
    want = (r >> 5) * HALF + f * ROWS_Y + ((r >> 3) & 3)
    return jnp.where((f < NF) & (c == want), 1.0, 0.0).astype(jnp.bfloat16)


def slot_relayout_back():
    r = lax.broadcasted_iota(jnp.int32, (PAIR, 64), 0)
    c = lax.broadcasted_iota(jnp.int32, (PAIR, 64), 1)
    f = c & 7
    want = (c >> 5) * HALF + f * ROWS_Y + ((c >> 3) & 3)
    return jnp.where((f < NF) & (r == want), 1.0, 0.0).astype(jnp.bfloat16)


def coupling(gas, motion, warmth, mass, weight):
    relative = [gas[k] - motion[k] for k in range(3)]
    speed_sq = relative[0] * relative[0] + relative[1] * relative[1] + relative[2] * relative[2]
    inv_surface = jnp.exp((-2.0 / 3.0) * jnp.log(mass))
    drag = 0.8 * (1.0 + 0.15 * jnp.exp(0.3435 * jnp.log(1.0 + speed_sq)))
    inverse_tau = drag * inv_surface
    relaxation = 1.0 - jnp.exp(-0.5 * inverse_tau)
    heating = 1.0 / (1.0 + jnp.exp(gas[4] - gas[3]))
    remain = jnp.exp(-0.3 * heating * inv_surface)
    new_mass = mass * remain
    warming = 1.0 - jnp.exp(-0.25 * inverse_tau)
    new_warmth = warmth + warming * (gas[3] - warmth) - 0.5 * (1.0 - remain)
    out = []
    for k in range(3):
        new_velocity = motion[k] + relaxation * relative[k]
        out.append(weight * (mass * motion[k] - new_mass * new_velocity))
    out.append(weight * (mass * warmth - new_mass * new_warmth))
    out.append(weight * (mass - new_mass))
    return out


STEP = 32
ENTRY_BITS = 11
ENTRY = 1 << ENTRY_BITS


def ordered_by_slot(slot, slots):
    lanes = slot.shape[1]
    spare = slots * ENTRY + slot.shape[0] * lanes
    slot_row = lax.broadcasted_iota(jnp.int32, (slots, lanes), 0)
    hits = [slot_row == jnp.broadcast_to(slot[r : r + 1], (slots, lanes)) for r in range(8)]
    p = lax.broadcasted_iota(jnp.int32, (lanes, 2 * lanes), 0)
    q = lax.broadcasted_iota(jnp.int32, (lanes, 2 * lanes), 1)
    upto = jnp.where(p <= q, 1.0, 0.0).astype(jnp.bfloat16)
    ones = jnp.concatenate([jnp.where(h, 1.0, 0.0).astype(jnp.bfloat16) for h in hits], axis=0)
    tally = jnp.dot(ones, upto, preferred_element_type=jnp.float32)
    count = sum(tally[slots * r : slots * (r + 1), lanes:] for r in range(8))
    pairs = ((count.astype(jnp.int32) + 1) >> 1)
    p = lax.broadcasted_iota(jnp.int32, (slots, slots), 0)
    q = lax.broadcasted_iota(jnp.int32, (slots, slots), 1)
    before = jnp.where(q < p, 1.0, 0.0).astype(jnp.bfloat16)
    halves = jnp.concatenate([(pairs >> 4).astype(jnp.float32), (pairs & 15).astype(jnp.float32)], axis=1)
    ahead = jnp.dot(before, halves.astype(jnp.bfloat16), preferred_element_type=jnp.float32)
    start = 2.0 * (16.0 * ahead[:, :lanes] + ahead[:, lanes:])
    number = start[slots - 1 :].astype(jnp.int32) + 2 * pairs[slots - 1 :]
    carry = start + (2 * STEP - 1.0)
    low = lax.broadcasted_iota(jnp.int32, (lanes, lanes), 0)
    high = lax.broadcasted_iota(jnp.int32, (16, lanes), 0)
    lane = lax.broadcasted_iota(jnp.int32, (16, lanes), 1).astype(jnp.float32)
    values, places = [], []
    for r in range(8):
        here = tally[slots * r : slots * (r + 1)]
        at = jnp.sum(jnp.where(hits[r], here[:, :lanes] + carry, 0.0), axis=0, keepdims=True)
        carry = carry + here[:, lanes:]
        own = slot[r : r + 1]
        at = jnp.where(own >= 0, at.astype(jnp.int32), -1)
        mask = high == (at >> 7)
        for_own = jnp.broadcast_to(own.astype(jnp.float32), (16, lanes))
        values.append(
            jnp.concatenate(
                [jnp.where(mask, v, 0.0) for v in (1.0, float(r), lane, for_own)], axis=0
            ).astype(jnp.bfloat16)
        )
        places.append(jnp.where(low == (at & (lanes - 1)), 1.0, 0.0).astype(jnp.bfloat16))
    found = lax.dot_general(
        jnp.concatenate(values, axis=1),
        jnp.concatenate(places, axis=1),
        NT,
        preferred_element_type=jnp.float32,
    )
    code = found[48:64] * float(ENTRY) + found[16:32] * float(lanes) + found[32:48]
    code = jnp.where(found[:16] > 0.5, code.astype(jnp.int32), spare)
    return jnp.where(high == 15, jnp.broadcast_to(number, (16, lanes)), code)


def couple_kernel(
    owners,
    blocks,
    live_ref,
    pick_ref,
    recv_ref,
    above_ref,
    below_ref,
    far_ref,
    cell_hbm,
    motion_hbm,
    warmth_hbm,
    mass_hbm,
    weight_hbm,
    out_ref,
    cell,
    motion,
    warmth,
    mass,
    weight,
    table,
    deposit,
    code_v,
    code_s,
    seen,
    gathered,
    source,
    sems,
):
    slots = 2 * owners
    copies = [
        pltpu.make_async_copy(a, b, sems.at[i])
        for i, (a, b) in enumerate(
            (
                (cell_hbm, cell.at[pl.ds(0, blocks)]),
                (motion_hbm, motion.at[:, pl.ds(0, blocks)]),
                (warmth_hbm, warmth.at[pl.ds(0, blocks)]),
                (mass_hbm, mass.at[pl.ds(0, blocks)]),
                (weight_hbm, weight.at[pl.ds(0, blocks)]),
            )
        )
    ]
    for copy in copies:
        copy.start()

    g = lax.axis_index("grp")
    counts = []
    for t in range(owners):
        first = recv_ref[t, :16].astype(jnp.float32)[:1]
        second = recv_ref[t, 16:32].astype(jnp.float32)[HALF - 16 : HALF - 15]
        held = jnp.where(first < EMPTY, 1.0, 0.0) + jnp.where(second < EMPTY, 1.0, 0.0)
        counts.append(jnp.broadcast_to(held, (8, LANES)))
    gas_groups = lax.axis_size("grp") - 1
    near_above = jnp.where(g >= 1, above_ref[...], 0.0)
    near_below = jnp.where(g < gas_groups - 1, below_ref[...], 0.0)
    far = jnp.where((g + 2) % lax.axis_size("grp") < gas_groups, far_ref[...], 0.0)
    total = sum(counts) + near_above + near_below + far
    before = near_above + jnp.where(g == gas_groups - 1, far, 0.0)
    divisor = jnp.maximum(total, 1.0)
    pick = pick_ref[...].astype(jnp.float32)
    quotient = (pick / divisor).astype(jnp.int32)
    divisor_int = divisor.astype(jnp.int32)
    picked = pick_ref[...] - quotient * divisor_int
    picked = jnp.where(picked < 0, picked + divisor_int, picked)
    picked = jnp.where(picked >= divisor_int, picked - divisor_int, picked)
    place = picked.astype(jnp.float32) - before
    running = jnp.zeros((8, LANES), jnp.float32)
    passed = jnp.zeros((8, LANES), jnp.float32)
    slot = jnp.zeros((8, LANES), jnp.float32)
    for t in range(owners):
        running = running + counts[t]
        beyond = running <= place
        slot = jnp.where(beyond, slot + 2.0, slot)
        passed = jnp.where(beyond, running, passed)
    slot = (slot + (place - passed)).astype(jnp.int32)
    block = (
        lax.broadcasted_iota(jnp.int32, (8, LANES), 0) * LANES
        + lax.broadcasted_iota(jnp.int32, (8, LANES), 1)
    )
    mine = (place >= 0.0) & (place < running) & (block < live_ref[0])
    code_v[...] = ordered_by_slot(jnp.where(mine, slot, -1), slots)
    to_scalar = pltpu.make_async_copy(code_v, code_s, sems.at[5])
    to_scalar.start()
    cell[blocks : blocks + 8] = jnp.zeros((8, LANES), jnp.int32)
    for k in range(3):
        motion[k, blocks : blocks + 8] = jnp.zeros((8, LANES), jnp.float32)
    warmth[blocks : blocks + 8] = jnp.zeros((8, LANES), jnp.float32)
    mass[blocks : blocks + 8] = jnp.ones((8, LANES), jnp.float32)
    weight[blocks : blocks + 8] = jnp.zeros((8, LANES), jnp.float32)

    spread = slot_relayout()
    for t in range(owners):
        rows = jnp.dot(spread, recv_ref[t], preferred_element_type=jnp.float32)
        table[8 * t : 8 * t + 8] = rows.reshape(8, 8, LANES)
    table[4 * slots : 4 * slots + 4] = jnp.zeros((4, 8, LANES), jnp.float32)

    def clear(t, carry):
        deposit[pl.ds(8 * t, 8)] = jnp.zeros((8, 8, LANES), jnp.float32)
        return carry

    lax.fori_loop(0, owners, clear, 0)
    deposit[4 * slots : 4 * slots + 4] = jnp.zeros((4, 8, LANES), jnp.float32)
    source[...] = jnp.zeros_like(source)
    to_scalar.wait()

    found = code_s[15, 0]
    for copy in copies:
        copy.wait()

    def entry(n0, i):
        code = code_s[n0 >> 7, (n0 & (LANES - 1)) + i]
        return code & (ENTRY - 1), code >> ENTRY_BITS

    cell_row = lax.broadcasted_iota(jnp.int32, (LANES, LANES), 0).astype(jnp.float32).astype(jnp.bfloat16)

    def look_up(j):
        n0 = STEP * j
        for i in range(0, STEP, 2):
            slot = entry(n0, i)[1]
            tile = [table[4 * slot + k] for k in range(ROWS_Y)]
            for h in range(2):
                b = entry(n0, i + h)[0]
                around = jnp.broadcast_to(cell[pl.ds(b, 1), :], (8, LANES))
                z, y = around & (LANES - 1), around >> 7
                rows = [jnp.take_along_axis(tile[k], z, axis=1) for k in range(ROWS_Y)]
                seen[i + h] = jnp.where(
                    y == 0, rows[0], jnp.where(y == 1, rows[1], jnp.where(y == 2, rows[2], rows[3]))
                )
                for k in range(3):
                    gathered[k, i + h : i + h + 1, :] = motion[k, pl.ds(b, 1), :]
                gathered[3, i + h : i + h + 1, :] = warmth[pl.ds(b, 1), :]
                gathered[4, i + h : i + h + 1, :] = mass[pl.ds(b, 1), :]
                gathered[5, i + h : i + h + 1, :] = weight[pl.ds(b, 1), :]

    def move():
        gas = [seen[:, f, :] for f in range(NF)]
        sources = coupling(
            gas,
            [gathered[k] for k in range(3)],
            gathered[3],
            gathered[4],
            gathered[5],
        )
        for f in range(NF):
            source[:, f, :] = sources[f]

    def scatter(j):
        n0 = STEP * j
        for i in range(0, STEP, 2):
            slot = entry(n0, i)[1]
            parts, hots = [], []
            for h in range(2):
                b = entry(n0, i + h)[0]
                cells = cell[pl.ds(b, 1), :]
                y = jnp.broadcast_to(cells, (8, LANES)) >> 7
                part = source[i + h]
                parts.append(
                    jnp.concatenate(
                        [jnp.where(y == k, part, 0.0) for k in range(ROWS_Y)], axis=0
                    ).astype(jnp.bfloat16)
                )
                hots.append(
                    jnp.where(cell_row == (cells & (LANES - 1)).astype(jnp.float32).astype(jnp.bfloat16), jnp.bfloat16(1), jnp.bfloat16(0))
                )
            added = lax.dot_general(
                jnp.concatenate(parts, axis=1),
                jnp.concatenate(hots, axis=1),
                NT,
                preferred_element_type=jnp.float32,
            ).reshape(4, 8, LANES)
            deposit[pl.ds(4 * slot, 4)] = deposit[pl.ds(4 * slot, 4)] + added

    def advance(j, carry):
        scatter(j)
        move()
        look_up(j + 2)
        return carry

    lax.fori_loop(0, (found + STEP - 1) // STEP + 2, advance, 0)

    back = slot_relayout_back()
    for t in range(owners):
        rows = deposit[8 * t : 8 * t + 8].reshape(64, LANES).astype(jnp.bfloat16)
        out_ref[t] = jnp.dot(back, rows, preferred_element_type=jnp.float32).astype(jnp.bfloat16)


def finish_kernel(
    planes,
    owners,
    holder_ref,
    flow_ref,
    nu_ref,
    xlo_ref,
    xhi_ref,
    up_ref,
    down_ref,
    landed_ref,
    out_ref,
    count,
    rows_above,
    rows_below,
):
    me = lax.axis_index("tile")
    g = lax.axis_index("grp")
    gas_groups = lax.axis_size("grp") - 1
    lane = lax.broadcasted_iota(jnp.int32, (ROWS_Y, LANES), 1)

    def clear(p, carry):
        count[p] = 0
        return carry

    lax.fori_loop(0, owners, clear, 0, unroll=True)

    rows_below[...] = up_ref[...].astype(jnp.float32)
    rows_above[...] = down_ref[...].astype(jnp.float32)
    xlo = [jnp.where(me > 0, xlo_ref[f], 0.0) for f in range(NF)]
    xhi = [jnp.where(me < owners - 1, xhi_ref[f], 0.0) for f in range(NF)]
    for x in range(planes):
        owner = holder_ref[x]
        rank = count[owner]
        count[owner] = rank + 1
        pair = landed_ref[owner].astype(jnp.float32)
        landed = jnp.where(rank == 0, pair[:HALF], pair[HALF : 2 * HALF])
        for f in range(NF):
            r = f * planes + x
            here = flow_ref[f, x]
            left = xlo[f] if x == 0 else flow_ref[f, x - 1]
            right = xhi[f] if x == planes - 1 else flow_ref[f, x + 1]
            first = jnp.where(g >= 1, rows_below[r : r + 1], 0.0)
            last = jnp.where(g < gas_groups - 1, rows_above[r : r + 1], 0.0)
            lower = jnp.concatenate([first, here[: ROWS_Y - 1]], axis=0)
            upper = jnp.concatenate([here[1:], last], axis=0)
            back = jnp.where(lane == 0, 0.0, pltpu.roll(here, 1, 1))
            ahead = jnp.where(lane == LANES - 1, 0.0, pltpu.roll(here, LANES - 1, 1))
            laplace = right + left + upper + lower + ahead + back - 6.0 * here
            value = here + 0.5 * nu_ref[x] * laplace + landed[ROWS_Y * f : ROWS_Y * f + ROWS_Y]
            out_ref[f, x] = jnp.where(g < gas_groups, value, 0.0)


def couple_call(live, pick, arrived, above, below, far, cell, motion, warmth, mass, weight):
    owners, blocks = arrived.shape[0], cell.shape[0]
    vmem = pl.BlockSpec(memory_space=pltpu.VMEM)
    smem = pl.BlockSpec(memory_space=pltpu.SMEM)
    hbm = pl.BlockSpec(memory_space=pl.ANY)
    params = pltpu.CompilerParams(vmem_limit_bytes=64136 * 1024)
    message = jax.ShapeDtypeStruct((owners, PAIR, LANES), jnp.bfloat16)

    def couple_body(*refs):
        couple_kernel(owners, blocks, *refs)

    return pl.pallas_call(
        couple_body,
        out_shape=message,
        in_specs=[smem] + [vmem] * 5 + [hbm] * 5,
        out_specs=vmem,
        scratch_shapes=[
            pltpu.VMEM((blocks + 8, LANES), jnp.int32),
            pltpu.VMEM((3, blocks + 8, LANES), jnp.float32),
            pltpu.VMEM((blocks + 8, LANES), jnp.float32),
            pltpu.VMEM((blocks + 8, LANES), jnp.float32),
            pltpu.VMEM((blocks + 8, LANES), jnp.float32),
            pltpu.VMEM((8 * owners + 4, 8, LANES), jnp.float32),
            pltpu.VMEM((8 * owners + 4, 8, LANES), jnp.float32),
            pltpu.VMEM((16, LANES), jnp.int32),
            pltpu.SMEM((16, LANES), jnp.int32),
            pltpu.VMEM((STEP, 8, LANES), jnp.float32),
            pltpu.VMEM((6, STEP, LANES), jnp.float32),
            pltpu.VMEM((STEP, 8, LANES), jnp.float32),
            pltpu.SemaphoreType.DMA((6,)),
        ],
        compiler_params=params,
    )(live, pick, arrived, above, below, far, cell, motion.transpose(1, 0, 2), warmth, mass, weight)


def local(
    flow_fields,
    turbulent_diffusivity,
    holder_unit,
    spray_volume_position,
    patch_pick_unreduced,
    droplet_motion,
    droplet_warmth,
    droplet_weightiness,
    droplet_multiplicity,
    living_spray_batches,
):
    groups = lax.axis_size("grp")
    owners = lax.axis_size("tile")
    planes = flow_fields.shape[1]
    blocks = spray_volume_position.shape[1]
    vmem = pl.BlockSpec(memory_space=pltpu.VMEM)
    smem = pl.BlockSpec(memory_space=pltpu.SMEM)
    params = pltpu.CompilerParams(vmem_limit_bytes=VMEM_LIMIT)

    holder = holder_unit.reshape(planes)

    def pack_body(*refs):
        pack_kernel(planes, owners, *refs)

    edge = jax.ShapeDtypeStruct((NF * planes, LANES), jnp.bfloat16)
    plane = jax.ShapeDtypeStruct((NF, ROWS_Y, LANES), jnp.float32)
    packed, top, bottom, front, behind = pl.pallas_call(
        pack_body,
        out_shape=(
            jax.ShapeDtypeStruct((owners, PAIR, LANES), jnp.bfloat16),
            edge,
            edge,
            plane,
            plane,
        ),
        in_specs=[smem, vmem],
        out_specs=(vmem,) * 5,
        scratch_shapes=[
            pltpu.SMEM((2 * owners,), jnp.int32),
            pltpu.SMEM((owners,), jnp.int32),
            pltpu.VMEM((NF * planes, LANES), jnp.float32),
            pltpu.VMEM((NF * planes, LANES), jnp.float32),
        ],
        compiler_params=params,
    )(holder, flow_fields)

    def turned(array, axis, step):
        size = lax.axis_size(axis)
        return lax.ppermute(array, axis, [(i, (i + step) % size) for i in range(size)])

    arrived = lax.all_to_all(packed, "tile", 0, 0, tiled=True)
    xlo = turned(behind, "tile", 1)
    xhi = turned(front, "tile", owners - 1)
    arrived, xlo, xhi = lax.optimization_barrier((arrived, xlo, xhi))

    held = (arrived[:, 0] < EMPTY).astype(jnp.float32) + (arrived[:, HALF] < EMPTY).astype(jnp.float32)
    number = jnp.broadcast_to(jnp.sum(held, axis=0), (8, LANES))
    above, far, below = (turned(number, "grp", k) for k in range(1, groups))

    outgoing = couple_call(
        living_spray_batches,
        patch_pick_unreduced.reshape(8, LANES),
        arrived,
        above,
        below,
        far,
        spray_volume_position[0],
        droplet_motion[0],
        droplet_warmth[0],
        droplet_weightiness[0],
        droplet_multiplicity[0],
    )

    outgoing, top, bottom = lax.optimization_barrier((outgoing, top, bottom))
    landed = lax.all_to_all(outgoing, "tile", 0, 0, tiled=True)
    up = turned(top, "grp", 1)
    down = turned(bottom, "grp", groups - 1)

    def finish_body(*refs):
        finish_kernel(planes, owners, *refs)

    return pl.pallas_call(
        finish_body,
        out_shape=jax.ShapeDtypeStruct(flow_fields.shape, jnp.float32),
        in_specs=[smem] + [vmem] * 7,
        out_specs=vmem,
        scratch_shapes=[
            pltpu.SMEM((owners,), jnp.int32),
            pltpu.VMEM((NF * planes, LANES), jnp.float32),
            pltpu.VMEM((NF * planes, LANES), jnp.float32),
        ],
        compiler_params=pltpu.CompilerParams(vmem_limit_bytes=40 * 1024 * 1024),
    )(holder, flow_fields, turbulent_diffusivity, xlo, xhi, up, down, landed)


def solution(mesh):
    in_specs = (
        P(None, "tile", "grp", None),
        P("tile", "grp", None),
        P("grp", "tile", None),
        P("tile", None, None),
        P("tile", None),
        P("tile", None, None, None),
        P("tile", None, None),
        P("tile", None, None),
        P("tile", None, None),
        P("tile"),
    )
    out_specs = P(None, "tile", "grp", None)
    return jax.shard_map(local, mesh=mesh, in_specs=in_specs, out_specs=out_specs, check_vma=False)
```

```python
import jax
import jax.numpy as jnp
from jax import lax
from jax.experimental import pallas as pl
from jax.experimental.pallas import tpu as pltpu
from jax.sharding import PartitionSpec as P

NF = 5
ROWS_Y = 4
LANES = 128
HALF = NF * ROWS_Y
PAIR = 2 * HALF
EMPTY = 2.0**100
VMEM_LIMIT = 65400 * 1024
NT = (((1,), (1,)), ((), ()))


def pack_kernel(
    planes,
    owners,
    holder_ref,
    flow_ref,
    out_ref,
    top_ref,
    bottom_ref,
    front_ref,
    back_ref,
    plane_of,
    count,
    rows_above,
    rows_below,
):
    is_gas = lax.axis_index("grp") < lax.axis_size("grp") - 1

    def clear(p, carry):
        count[p] = 0
        plane_of[2 * p] = 0
        plane_of[2 * p + 1] = 0
        return carry

    lax.fori_loop(0, owners, clear, 0, unroll=True)

    def place(x, carry):
        owner = holder_ref[x]
        rank = count[owner]
        plane_of[2 * owner + jnp.minimum(rank, 1)] = x
        count[owner] = rank + 1
        return carry

    lax.fori_loop(0, planes, place, 0, unroll=True)

    row = lax.broadcasted_iota(jnp.int32, (PAIR, LANES), 0)
    for p in range(owners):
        pieces = []
        for s in range(2):
            x = plane_of[2 * p + s]
            pieces += [flow_ref[f, x] for f in range(NF)]
        filled = HALF * jnp.where(is_gas, count[p], 0)
        rows = jnp.where(row < filled, jnp.concatenate(pieces, axis=0), EMPTY)
        out_ref[p] = rows.astype(jnp.bfloat16)

    for f in range(NF):
        for x in range(planes):
            r = f * planes + x
            rows_above[r : r + 1] = flow_ref[f, x, ROWS_Y - 1 :]
            rows_below[r : r + 1] = flow_ref[f, x, :1]
        front_ref[f] = flow_ref[f, 0]
        back_ref[f] = flow_ref[f, planes - 1]
    top_ref[...] = rows_above[...].astype(jnp.bfloat16)
    bottom_ref[...] = rows_below[...].astype(jnp.bfloat16)


def slot_relayout():
    r = lax.broadcasted_iota(jnp.int32, (64, PAIR), 0)
    c = lax.broadcasted_iota(jnp.int32, (64, PAIR), 1)
    f = r & 7
    want = (r >> 5) * HALF + f * ROWS_Y + ((r >> 3) & 3)
    return jnp.where((f < NF) & (c == want), 1.0, 0.0).astype(jnp.bfloat16)


def slot_relayout_back():
    r = lax.broadcasted_iota(jnp.int32, (PAIR, 64), 0)
    c = lax.broadcasted_iota(jnp.int32, (PAIR, 64), 1)
    f = c & 7
    want = (c >> 5) * HALF + f * ROWS_Y + ((c >> 3) & 3)
    return jnp.where((f < NF) & (r == want), 1.0, 0.0).astype(jnp.bfloat16)


def coupling(gas, motion, warmth, mass, weight):
    relative = [gas[k] - motion[k] for k in range(3)]
    speed_sq = relative[0] * relative[0] + relative[1] * relative[1] + relative[2] * relative[2]
    inv_surface = jnp.exp((-2.0 / 3.0) * jnp.log(mass))
    drag = 0.8 * (1.0 + 0.15 * jnp.exp(0.3435 * jnp.log(1.0 + speed_sq)))
    inverse_tau = drag * inv_surface
    relaxation = 1.0 - jnp.exp(-0.5 * inverse_tau)
    heating = 1.0 / (1.0 + jnp.exp(gas[4] - gas[3]))
    remain = jnp.exp(-0.3 * heating * inv_surface)
    new_mass = mass * remain
    warming = 1.0 - jnp.exp(-0.25 * inverse_tau)
    new_warmth = warmth + warming * (gas[3] - warmth) - 0.5 * (1.0 - remain)
    out = []
    for k in range(3):
        new_velocity = motion[k] + relaxation * relative[k]
        out.append(weight * (mass * motion[k] - new_mass * new_velocity))
    out.append(weight * (mass * warmth - new_mass * new_warmth))
    out.append(weight * (mass - new_mass))
    return out


STEP = 32
ENTRY_BITS = 11
ENTRY = 1 << ENTRY_BITS


def ordered_by_slot(slot, slots):
    lanes = slot.shape[1]
    spare = slots * ENTRY + slot.shape[0] * lanes
    slot_row = lax.broadcasted_iota(jnp.int32, (slots, lanes), 0)
    hits = [slot_row == jnp.broadcast_to(slot[r : r + 1], (slots, lanes)) for r in range(8)]
    p = lax.broadcasted_iota(jnp.int32, (lanes, 2 * lanes), 0)
    q = lax.broadcasted_iota(jnp.int32, (lanes, 2 * lanes), 1)
    upto = jnp.where(p <= q, 1.0, 0.0).astype(jnp.bfloat16)
    ones = jnp.concatenate([jnp.where(h, 1.0, 0.0).astype(jnp.bfloat16) for h in hits], axis=0)
    tally = jnp.dot(ones, upto, preferred_element_type=jnp.float32)
    count = sum(tally[slots * r : slots * (r + 1), lanes:] for r in range(8))
    pairs = ((count.astype(jnp.int32) + 1) >> 1)
    p = lax.broadcasted_iota(jnp.int32, (slots, slots), 0)
    q = lax.broadcasted_iota(jnp.int32, (slots, slots), 1)
    before = jnp.where(q < p, 1.0, 0.0).astype(jnp.bfloat16)
    halves = jnp.concatenate([(pairs >> 4).astype(jnp.float32), (pairs & 15).astype(jnp.float32)], axis=1)
    ahead = jnp.dot(before, halves.astype(jnp.bfloat16), preferred_element_type=jnp.float32)
    start = 2.0 * (16.0 * ahead[:, :lanes] + ahead[:, lanes:])
    number = start[slots - 1 :].astype(jnp.int32) + 2 * pairs[slots - 1 :]
    carry = start + (2 * STEP - 1.0)
    low = lax.broadcasted_iota(jnp.int32, (lanes, lanes), 0)
    high = lax.broadcasted_iota(jnp.int32, (16, lanes), 0)
    lane = lax.broadcasted_iota(jnp.int32, (16, lanes), 1).astype(jnp.float32)
    values, places = [], []
    for r in range(8):
        here = tally[slots * r : slots * (r + 1)]
        at = jnp.sum(jnp.where(hits[r], here[:, :lanes] + carry, 0.0), axis=0, keepdims=True)
        carry = carry + here[:, lanes:]
        own = slot[r : r + 1]
        at = jnp.where(own >= 0, at.astype(jnp.int32), -1)
        mask = high == (at >> 7)
        for_own = jnp.broadcast_to(own.astype(jnp.float32), (16, lanes))
        values.append(
            jnp.concatenate(
                [jnp.where(mask, v, 0.0) for v in (1.0, float(r), lane, for_own)], axis=0
            ).astype(jnp.bfloat16)
        )
        places.append(jnp.where(low == (at & (lanes - 1)), 1.0, 0.0).astype(jnp.bfloat16))
    found = lax.dot_general(
        jnp.concatenate(values, axis=1),
        jnp.concatenate(places, axis=1),
        NT,
        preferred_element_type=jnp.float32,
    )
    code = found[48:64] * float(ENTRY) + found[16:32] * float(lanes) + found[32:48]
    code = jnp.where(found[:16] > 0.5, code.astype(jnp.int32), spare)
    return jnp.where(high == 15, jnp.broadcast_to(number, (16, lanes)), code)


def couple_kernel(
    owners,
    blocks,
    live_ref,
    pick_ref,
    recv_ref,
    above_ref,
    below_ref,
    far_ref,
    cell_hbm,
    motion_hbm,
    warmth_hbm,
    mass_hbm,
    weight_hbm,
    out_ref,
    cell,
    motion,
    warmth,
    mass,
    weight,
    table,
    deposit,
    code_v,
    code_s,
    seen,
    gathered,
    source,
    sems,
):
    slots = 2 * owners
    copies = [
        pltpu.make_async_copy(a, b, sems.at[i])
        for i, (a, b) in enumerate(
            (
                (cell_hbm, cell.at[pl.ds(0, blocks)]),
                (motion_hbm, motion.at[:, pl.ds(0, blocks)]),
                (warmth_hbm, warmth.at[pl.ds(0, blocks)]),
                (mass_hbm, mass.at[pl.ds(0, blocks)]),
                (weight_hbm, weight.at[pl.ds(0, blocks)]),
            )
        )
    ]
    for copy in copies:
        copy.start()

    g = lax.axis_index("grp")
    counts = []
    for t in range(owners):
        first = recv_ref[t, :16].astype(jnp.float32)[:1]
        second = recv_ref[t, 16:32].astype(jnp.float32)[HALF - 16 : HALF - 15]
        held = jnp.where(first < EMPTY, 1.0, 0.0) + jnp.where(second < EMPTY, 1.0, 0.0)
        counts.append(jnp.broadcast_to(held, (8, LANES)))
    gas_groups = lax.axis_size("grp") - 1
    near_above = jnp.where(g >= 1, above_ref[...], 0.0)
    near_below = jnp.where(g < gas_groups - 1, below_ref[...], 0.0)
    far = jnp.where((g + 2) % lax.axis_size("grp") < gas_groups, far_ref[...], 0.0)
    total = sum(counts) + near_above + near_below + far
    before = near_above + jnp.where(g == gas_groups - 1, far, 0.0)
    divisor = jnp.maximum(total, 1.0)
    pick = pick_ref[...]
    quotient = (pick / divisor).astype(jnp.int32)
    divisor_int = divisor.astype(jnp.int32)
    picked = pick.astype(jnp.int32) - quotient * divisor_int
    picked = jnp.where(picked < 0, picked + divisor_int, picked)
    picked = jnp.where(picked >= divisor_int, picked - divisor_int, picked)
    place = picked.astype(jnp.float32) - before
    running = jnp.zeros((8, LANES), jnp.float32)
    passed = jnp.zeros((8, LANES), jnp.float32)
    slot = jnp.zeros((8, LANES), jnp.float32)
    for t in range(owners):
        running = running + counts[t]
        beyond = running <= place
        slot = jnp.where(beyond, slot + 2.0, slot)
        passed = jnp.where(beyond, running, passed)
    slot = (slot + (place - passed)).astype(jnp.int32)
    block = (
        lax.broadcasted_iota(jnp.int32, (8, LANES), 0) * LANES
        + lax.broadcasted_iota(jnp.int32, (8, LANES), 1)
    )
    mine = (place >= 0.0) & (place < running) & (block < live_ref[0])
    code_v[...] = ordered_by_slot(jnp.where(mine, slot, -1), slots)
    to_scalar = pltpu.make_async_copy(code_v, code_s, sems.at[5])
    to_scalar.start()
    cell[blocks : blocks + 8] = jnp.zeros((8, LANES), jnp.int32)
    for k in range(3):
        motion[k, blocks : blocks + 8] = jnp.zeros((8, LANES), jnp.float32)
    warmth[blocks : blocks + 8] = jnp.zeros((8, LANES), jnp.float32)
    mass[blocks : blocks + 8] = jnp.ones((8, LANES), jnp.float32)
    weight[blocks : blocks + 8] = jnp.zeros((8, LANES), jnp.float32)

    spread = slot_relayout()
    for t in range(owners):
        rows = jnp.dot(spread, recv_ref[t], preferred_element_type=jnp.float32)
        table[8 * t : 8 * t + 8] = rows.reshape(8, 8, LANES)
    table[4 * slots : 4 * slots + 4] = jnp.zeros((4, 8, LANES), jnp.float32)

    def clear(t, carry):
        deposit[pl.ds(8 * t, 8)] = jnp.zeros((8, 8, LANES), jnp.float32)
        return carry

    lax.fori_loop(0, owners, clear, 0)
    deposit[4 * slots : 4 * slots + 4] = jnp.zeros((4, 8, LANES), jnp.float32)
    source[...] = jnp.zeros_like(source)
    to_scalar.wait()

    found = code_s[15, 0]
    for copy in copies:
        copy.wait()

    def entry(n0, i):
        code = code_s[n0 >> 7, (n0 & (LANES - 1)) + i]
        return code & (ENTRY - 1), code >> ENTRY_BITS

    cell_row = lax.broadcasted_iota(jnp.int32, (LANES, LANES), 0).astype(jnp.float32).astype(jnp.bfloat16)

    def look_up(j):
        n0 = STEP * j
        for i in range(0, STEP, 2):
            slot = entry(n0, i)[1]
            tile = [table[4 * slot + k] for k in range(ROWS_Y)]
            for h in range(2):
                b = entry(n0, i + h)[0]
                around = jnp.broadcast_to(cell[pl.ds(b, 1), :], (8, LANES))
                z, y = around & (LANES - 1), around >> 7
                rows = [jnp.take_along_axis(tile[k], z, axis=1) for k in range(ROWS_Y)]
                seen[i + h] = jnp.where(
                    y == 0, rows[0], jnp.where(y == 1, rows[1], jnp.where(y == 2, rows[2], rows[3]))
                )
                for k in range(3):
                    gathered[k, i + h : i + h + 1, :] = motion[k, pl.ds(b, 1), :]
                gathered[3, i + h : i + h + 1, :] = warmth[pl.ds(b, 1), :]
                gathered[4, i + h : i + h + 1, :] = mass[pl.ds(b, 1), :]
                gathered[5, i + h : i + h + 1, :] = weight[pl.ds(b, 1), :]

    def move():
        gas = [seen[:, f, :] for f in range(NF)]
        sources = coupling(
            gas,
            [gathered[k] for k in range(3)],
            gathered[3],
            gathered[4],
            gathered[5],
        )
        for f in range(NF):
            source[:, f, :] = sources[f]

    def scatter(j):
        n0 = STEP * j
        for i in range(0, STEP, 2):
            slot = entry(n0, i)[1]
            parts, hots = [], []
            for h in range(2):
                b = entry(n0, i + h)[0]
                cells = cell[pl.ds(b, 1), :]
                y = jnp.broadcast_to(cells, (8, LANES)) >> 7
                part = source[i + h]
                parts.append(
                    jnp.concatenate(
                        [jnp.where(y == k, part, 0.0) for k in range(ROWS_Y)], axis=0
                    ).astype(jnp.bfloat16)
                )
                hots.append(
                    jnp.where(cell_row == (cells & (LANES - 1)).astype(jnp.float32).astype(jnp.bfloat16), jnp.bfloat16(1), jnp.bfloat16(0))
                )
            added = lax.dot_general(
                jnp.concatenate(parts, axis=1),
                jnp.concatenate(hots, axis=1),
                NT,
                preferred_element_type=jnp.float32,
            ).reshape(4, 8, LANES)
            deposit[pl.ds(4 * slot, 4)] = deposit[pl.ds(4 * slot, 4)] + added

    def advance(j, carry):
        scatter(j)
        move()
        look_up(j + 2)
        return carry

    lax.fori_loop(0, (found + STEP - 1) // STEP + 2, advance, 0)

    back = slot_relayout_back()
    for t in range(owners):
        rows = deposit[8 * t : 8 * t + 8].reshape(64, LANES).astype(jnp.bfloat16)
        out_ref[t] = jnp.dot(back, rows, preferred_element_type=jnp.float32).astype(jnp.bfloat16)


def finish_kernel(
    planes,
    owners,
    holder_ref,
    flow_ref,
    nu_ref,
    xlo_ref,
    xhi_ref,
    up_ref,
    down_ref,
    landed_ref,
    out_ref,
    count,
    rows_above,
    rows_below,
):
    me = lax.axis_index("tile")
    g = lax.axis_index("grp")
    gas_groups = lax.axis_size("grp") - 1
    lane = lax.broadcasted_iota(jnp.int32, (ROWS_Y, LANES), 1)

    def clear(p, carry):
        count[p] = 0
        return carry

    lax.fori_loop(0, owners, clear, 0, unroll=True)

    rows_below[...] = up_ref[...].astype(jnp.float32)
    rows_above[...] = down_ref[...].astype(jnp.float32)
    xlo = [jnp.where(me > 0, xlo_ref[f], 0.0) for f in range(NF)]
    xhi = [jnp.where(me < owners - 1, xhi_ref[f], 0.0) for f in range(NF)]
    for x in range(planes):
        owner = holder_ref[x]
        rank = count[owner]
        count[owner] = rank + 1
        pair = landed_ref[owner].astype(jnp.float32)
        landed = jnp.where(rank == 0, pair[:HALF], pair[HALF : 2 * HALF])
        for f in range(NF):
            r = f * planes + x
            here = flow_ref[f, x]
            left = xlo[f] if x == 0 else flow_ref[f, x - 1]
            right = xhi[f] if x == planes - 1 else flow_ref[f, x + 1]
            first = jnp.where(g >= 1, rows_below[r : r + 1], 0.0)
            last = jnp.where(g < gas_groups - 1, rows_above[r : r + 1], 0.0)
            lower = jnp.concatenate([first, here[: ROWS_Y - 1]], axis=0)
            upper = jnp.concatenate([here[1:], last], axis=0)
            back = jnp.where(lane == 0, 0.0, pltpu.roll(here, 1, 1))
            ahead = jnp.where(lane == LANES - 1, 0.0, pltpu.roll(here, LANES - 1, 1))
            laplace = right + left + upper + lower + ahead + back - 6.0 * here
            value = here + 0.5 * nu_ref[x] * laplace + landed[ROWS_Y * f : ROWS_Y * f + ROWS_Y]
            out_ref[f, x] = jnp.where(g < gas_groups, value, 0.0)


def couple_call(live, pick, arrived, above, below, far, cell, motion, warmth, mass, weight):
    owners, blocks = arrived.shape[0], cell.shape[0]
    vmem = pl.BlockSpec(memory_space=pltpu.VMEM)
    smem = pl.BlockSpec(memory_space=pltpu.SMEM)
    hbm = pl.BlockSpec(memory_space=pl.ANY)
    params = pltpu.CompilerParams(vmem_limit_bytes=54336 * 1024)
    message = jax.ShapeDtypeStruct((owners, PAIR, LANES), jnp.bfloat16)

    def couple_body(*refs):
        couple_kernel(owners, blocks, *refs)

    return pl.pallas_call(
        couple_body,
        out_shape=message,
        in_specs=[smem] + [vmem] * 5 + [hbm] * 5,
        out_specs=vmem,
        scratch_shapes=[
            pltpu.VMEM((blocks + 8, LANES), jnp.int32),
            pltpu.VMEM((3, blocks + 8, LANES), jnp.float32),
            pltpu.VMEM((blocks + 8, LANES), jnp.float32),
            pltpu.VMEM((blocks + 8, LANES), jnp.float32),
            pltpu.VMEM((blocks + 8, LANES), jnp.float32),
            pltpu.VMEM((8 * owners + 4, 8, LANES), jnp.float32),
            pltpu.VMEM((8 * owners + 4, 8, LANES), jnp.float32),
            pltpu.VMEM((16, LANES), jnp.int32),
            pltpu.SMEM((16, LANES), jnp.int32),
            pltpu.VMEM((STEP, 8, LANES), jnp.float32),
            pltpu.VMEM((6, STEP, LANES), jnp.float32),
            pltpu.VMEM((STEP, 8, LANES), jnp.float32),
            pltpu.SemaphoreType.DMA((6,)),
        ],
        compiler_params=params,
    )(live, pick, arrived, above, below, far, cell, motion.transpose(1, 0, 2), warmth, mass, weight)


def local(
    flow_fields,
    turbulent_diffusivity,
    holder_unit,
    spray_volume_position,
    patch_pick_unreduced,
    droplet_motion,
    droplet_warmth,
    droplet_weightiness,
    droplet_multiplicity,
    living_spray_batches,
):
    groups = lax.axis_size("grp")
    owners = lax.axis_size("tile")
    planes = flow_fields.shape[1]
    blocks = spray_volume_position.shape[1]
    vmem = pl.BlockSpec(memory_space=pltpu.VMEM)
    smem = pl.BlockSpec(memory_space=pltpu.SMEM)
    params = pltpu.CompilerParams(vmem_limit_bytes=VMEM_LIMIT)

    holder = holder_unit.reshape(planes)

    def pack_body(*refs):
        pack_kernel(planes, owners, *refs)

    edge = jax.ShapeDtypeStruct((NF * planes, LANES), jnp.bfloat16)
    plane = jax.ShapeDtypeStruct((NF, ROWS_Y, LANES), jnp.float32)
    packed, top, bottom, front, behind = pl.pallas_call(
        pack_body,
        out_shape=(
            jax.ShapeDtypeStruct((owners, PAIR, LANES), jnp.bfloat16),
            edge,
            edge,
            plane,
            plane,
        ),
        in_specs=[smem, vmem],
        out_specs=(vmem,) * 5,
        scratch_shapes=[
            pltpu.SMEM((2 * owners,), jnp.int32),
            pltpu.SMEM((owners,), jnp.int32),
            pltpu.VMEM((NF * planes, LANES), jnp.float32),
            pltpu.VMEM((NF * planes, LANES), jnp.float32),
        ],
        compiler_params=params,
    )(holder, flow_fields)

    def turned(array, axis, step):
        size = lax.axis_size(axis)
        return lax.ppermute(array, axis, [(i, (i + step) % size) for i in range(size)])

    arrived = lax.all_to_all(packed, "tile", 0, 0, tiled=True)
    xlo = turned(behind, "tile", 1)
    xhi = turned(front, "tile", owners - 1)
    pick = patch_pick_unreduced.reshape(8, LANES).astype(jnp.float32)
    arrived, xlo, xhi, pick = lax.optimization_barrier((arrived, xlo, xhi, pick))

    held = (arrived[:, 0] < EMPTY).astype(jnp.float32) + (arrived[:, HALF] < EMPTY).astype(jnp.float32)
    number = jnp.broadcast_to(jnp.sum(held, axis=0), (8, LANES))
    above, far, below = (turned(number, "grp", k) for k in range(1, groups))

    outgoing = couple_call(
        living_spray_batches,
        pick,
        arrived,
        above,
        below,
        far,
        spray_volume_position[0],
        droplet_motion[0],
        droplet_warmth[0],
        droplet_weightiness[0],
        droplet_multiplicity[0],
    )

    outgoing, top, bottom = lax.optimization_barrier((outgoing, top, bottom))
    landed = lax.all_to_all(outgoing, "tile", 0, 0, tiled=True)
    up = turned(top, "grp", 1)
    down = turned(bottom, "grp", groups - 1)

    def finish_body(*refs):
        finish_kernel(planes, owners, *refs)

    return pl.pallas_call(
        finish_body,
        out_shape=jax.ShapeDtypeStruct(flow_fields.shape, jnp.float32),
        in_specs=[smem] + [vmem] * 7,
        out_specs=vmem,
        scratch_shapes=[
            pltpu.SMEM((owners,), jnp.int32),
            pltpu.VMEM((NF * planes, LANES), jnp.float32),
            pltpu.VMEM((NF * planes, LANES), jnp.float32),
        ],
        compiler_params=pltpu.CompilerParams(vmem_limit_bytes=40 * 1024 * 1024),
    )(holder, flow_fields, turbulent_diffusivity, xlo, xhi, up, down, landed)


def solution(mesh):
    in_specs = (
        P(None, "tile", "grp", None),
        P("tile", "grp", None),
        P("grp", "tile", None),
        P("tile", None, None),
        P("tile", None),
        P("tile", None, None, None),
        P("tile", None, None),
        P("tile", None, None),
        P("tile", None, None),
        P("tile"),
    )
    out_specs = P(None, "tile", "grp", None)
    return jax.shard_map(local, mesh=mesh, in_specs=in_specs, out_specs=out_specs, check_vma=False)
```

```python
import jax
import jax.numpy as jnp
from jax import lax
from jax.experimental import pallas as pl
from jax.experimental.pallas import tpu as pltpu
from jax.sharding import PartitionSpec as P

NF = 5
ROWS_Y = 4
LANES = 128
HALF = NF * ROWS_Y
PAIR = 2 * HALF
EMPTY = 2.0**100
VMEM_LIMIT = 65400 * 1024
NT = (((1,), (1,)), ((), ()))


def pack_kernel(
    planes,
    owners,
    holder_ref,
    flow_ref,
    out_ref,
    top_ref,
    bottom_ref,
    front_ref,
    back_ref,
    plane_of,
    count,
    rows_above,
    rows_below,
):
    is_gas = lax.axis_index("grp") < lax.axis_size("grp") - 1

    def clear(p, carry):
        count[p] = 0
        plane_of[2 * p] = 0
        plane_of[2 * p + 1] = 0
        return carry

    lax.fori_loop(0, owners, clear, 0, unroll=True)

    def place(x, carry):
        owner = holder_ref[x]
        rank = count[owner]
        plane_of[2 * owner + jnp.minimum(rank, 1)] = x
        count[owner] = rank + 1
        return carry

    lax.fori_loop(0, planes, place, 0, unroll=True)

    row = lax.broadcasted_iota(jnp.int32, (PAIR, LANES), 0)
    for p in range(owners):
        pieces = []
        for s in range(2):
            x = plane_of[2 * p + s]
            pieces += [flow_ref[f, x] for f in range(NF)]
        filled = HALF * jnp.where(is_gas, count[p], 0)
        rows = jnp.where(row < filled, jnp.concatenate(pieces, axis=0), EMPTY)
        out_ref[p] = rows.astype(jnp.bfloat16)

    for f in range(NF):
        for x in range(planes):
            r = f * planes + x
            rows_above[r : r + 1] = flow_ref[f, x, ROWS_Y - 1 :]
            rows_below[r : r + 1] = flow_ref[f, x, :1]
        front_ref[f] = flow_ref[f, 0]
        back_ref[f] = flow_ref[f, planes - 1]
    top_ref[...] = rows_above[...].astype(jnp.bfloat16)
    bottom_ref[...] = rows_below[...].astype(jnp.bfloat16)


def slot_relayout():
    r = lax.broadcasted_iota(jnp.int32, (64, PAIR), 0)
    c = lax.broadcasted_iota(jnp.int32, (64, PAIR), 1)
    f = r & 7
    want = (r >> 5) * HALF + f * ROWS_Y + ((r >> 3) & 3)
    return jnp.where((f < NF) & (c == want), 1.0, 0.0).astype(jnp.bfloat16)


def slot_relayout_back():
    r = lax.broadcasted_iota(jnp.int32, (PAIR, 64), 0)
    c = lax.broadcasted_iota(jnp.int32, (PAIR, 64), 1)
    f = c & 7
    want = (c >> 5) * HALF + f * ROWS_Y + ((c >> 3) & 3)
    return jnp.where((f < NF) & (r == want), 1.0, 0.0).astype(jnp.bfloat16)


def coupling(gas, motion, warmth, mass, weight):
    relative = [gas[k] - motion[k] for k in range(3)]
    speed_sq = relative[0] * relative[0] + relative[1] * relative[1] + relative[2] * relative[2]
    inv_surface = jnp.exp((-2.0 / 3.0) * jnp.log(mass))
    drag = 0.8 * (1.0 + 0.15 * jnp.exp(0.3435 * jnp.log(1.0 + speed_sq)))
    inverse_tau = drag * inv_surface
    relaxation = 1.0 - jnp.exp(-0.5 * inverse_tau)
    heating = 1.0 / (1.0 + jnp.exp(gas[4] - gas[3]))
    remain = jnp.exp(-0.3 * heating * inv_surface)
    new_mass = mass * remain
    warming = 1.0 - jnp.exp(-0.25 * inverse_tau)
    new_warmth = warmth + warming * (gas[3] - warmth) - 0.5 * (1.0 - remain)
    out = []
    for k in range(3):
        new_velocity = motion[k] + relaxation * relative[k]
        out.append(weight * (mass * motion[k] - new_mass * new_velocity))
    out.append(weight * (mass * warmth - new_mass * new_warmth))
    out.append(weight * (mass - new_mass))
    return out


STEP = 32
ENTRY_BITS = 11
ENTRY = 1 << ENTRY_BITS


def ordered_by_slot(slot, slots):
    lanes = slot.shape[1]
    spare = slots * ENTRY + slot.shape[0] * lanes
    slot_row = lax.broadcasted_iota(jnp.int32, (slots, lanes), 0)
    hits = [slot_row == jnp.broadcast_to(slot[r : r + 1], (slots, lanes)) for r in range(8)]
    p = lax.broadcasted_iota(jnp.int32, (lanes, 2 * lanes), 0)
    q = lax.broadcasted_iota(jnp.int32, (lanes, 2 * lanes), 1)
    upto = jnp.where(p <= q, 1.0, 0.0).astype(jnp.bfloat16)
    ones = jnp.concatenate([jnp.where(h, 1.0, 0.0).astype(jnp.bfloat16) for h in hits], axis=0)
    tally = jnp.dot(ones, upto, preferred_element_type=jnp.float32)
    count = sum(tally[slots * r : slots * (r + 1), lanes:] for r in range(8))
    pairs = ((count.astype(jnp.int32) + 1) >> 1)
    p = lax.broadcasted_iota(jnp.int32, (slots, slots), 0)
    q = lax.broadcasted_iota(jnp.int32, (slots, slots), 1)
    before = jnp.where(q < p, 1.0, 0.0).astype(jnp.bfloat16)
    halves = jnp.concatenate([(pairs >> 4).astype(jnp.float32), (pairs & 15).astype(jnp.float32)], axis=1)
    ahead = jnp.dot(before, halves.astype(jnp.bfloat16), preferred_element_type=jnp.float32)
    start = 2.0 * (16.0 * ahead[:, :lanes] + ahead[:, lanes:])
    number = start[slots - 1 :].astype(jnp.int32) + 2 * pairs[slots - 1 :]
    carry = start + (STEP - 1.0)
    low = lax.broadcasted_iota(jnp.int32, (lanes, lanes), 0)
    high = lax.broadcasted_iota(jnp.int32, (16, lanes), 0)
    lane = lax.broadcasted_iota(jnp.int32, (16, lanes), 1).astype(jnp.float32)
    values, places = [], []
    for r in range(8):
        here = tally[slots * r : slots * (r + 1)]
        at = jnp.sum(jnp.where(hits[r], here[:, :lanes] + carry, 0.0), axis=0, keepdims=True)
        carry = carry + here[:, lanes:]
        own = slot[r : r + 1]
        at = jnp.where(own >= 0, at.astype(jnp.int32), -1)
        mask = high == (at >> 7)
        for_own = jnp.broadcast_to(own.astype(jnp.float32), (16, lanes))
        values.append(
            jnp.concatenate(
                [jnp.where(mask, v, 0.0) for v in (1.0, float(r), lane, for_own)], axis=0
            ).astype(jnp.bfloat16)
        )
        places.append(jnp.where(low == (at & (lanes - 1)), 1.0, 0.0).astype(jnp.bfloat16))
    found = lax.dot_general(
        jnp.concatenate(values, axis=1),
        jnp.concatenate(places, axis=1),
        NT,
        preferred_element_type=jnp.float32,
    )
    code = found[48:64] * float(ENTRY) + found[16:32] * float(lanes) + found[32:48]
    code = jnp.where(found[:16] > 0.5, code.astype(jnp.int32), spare)
    return jnp.where(high == 15, jnp.broadcast_to(number, (16, lanes)), code)


def couple_kernel(
    owners,
    blocks,
    live_ref,
    pick_ref,
    recv_ref,
    above_ref,
    below_ref,
    far_ref,
    cell_hbm,
    motion_hbm,
    warmth_hbm,
    mass_hbm,
    weight_hbm,
    out_ref,
    cell,
    motion,
    warmth,
    mass,
    weight,
    table,
    deposit,
    code_v,
    code_s,
    seen,
    gathered,
    source,
    sems,
):
    slots = 2 * owners
    copies = [
        pltpu.make_async_copy(a, b, sems.at[i])
        for i, (a, b) in enumerate(
            (
                (cell_hbm, cell.at[pl.ds(0, blocks)]),
                (motion_hbm, motion.at[:, pl.ds(0, blocks)]),
                (warmth_hbm, warmth.at[pl.ds(0, blocks)]),
                (mass_hbm, mass.at[pl.ds(0, blocks)]),
                (weight_hbm, weight.at[pl.ds(0, blocks)]),
            )
        )
    ]
    for copy in copies:
        copy.start()

    g = lax.axis_index("grp")
    counts = []
    for t in range(owners):
        first = recv_ref[t, :16].astype(jnp.float32)[:1]
        second = recv_ref[t, 16:32].astype(jnp.float32)[HALF - 16 : HALF - 15]
        held = jnp.where(first < EMPTY, 1.0, 0.0) + jnp.where(second < EMPTY, 1.0, 0.0)
        counts.append(jnp.broadcast_to(held, (8, LANES)))
    gas_groups = lax.axis_size("grp") - 1
    near_above = jnp.where(g >= 1, above_ref[...], 0.0)
    near_below = jnp.where(g < gas_groups - 1, below_ref[...], 0.0)
    far = jnp.where((g + 2) % lax.axis_size("grp") < gas_groups, far_ref[...], 0.0)
    total = sum(counts) + near_above + near_below + far
    before = near_above + jnp.where(g == gas_groups - 1, far, 0.0)
    divisor = jnp.maximum(total, 1.0)
    pick = pick_ref[...]
    quotient = (pick / divisor).astype(jnp.int32)
    divisor_int = divisor.astype(jnp.int32)
    picked = pick.astype(jnp.int32) - quotient * divisor_int
    picked = jnp.where(picked < 0, picked + divisor_int, picked)
    picked = jnp.where(picked >= divisor_int, picked - divisor_int, picked)
    place = picked.astype(jnp.float32) - before
    running = jnp.zeros((8, LANES), jnp.float32)
    passed = jnp.zeros((8, LANES), jnp.float32)
    slot = jnp.zeros((8, LANES), jnp.float32)
    for t in range(owners):
        running = running + counts[t]
        beyond = running <= place
        slot = jnp.where(beyond, slot + 2.0, slot)
        passed = jnp.where(beyond, running, passed)
    slot = (slot + (place - passed)).astype(jnp.int32)
    block = (
        lax.broadcasted_iota(jnp.int32, (8, LANES), 0) * LANES
        + lax.broadcasted_iota(jnp.int32, (8, LANES), 1)
    )
    mine = (place >= 0.0) & (place < running) & (block < live_ref[0])
    code_v[...] = ordered_by_slot(jnp.where(mine, slot, -1), slots)
    to_scalar = pltpu.make_async_copy(code_v, code_s, sems.at[5])
    to_scalar.start()
    cell[blocks : blocks + 8] = jnp.zeros((8, LANES), jnp.int32)
    for k in range(3):
        motion[k, blocks : blocks + 8] = jnp.zeros((8, LANES), jnp.float32)
    warmth[blocks : blocks + 8] = jnp.zeros((8, LANES), jnp.float32)
    mass[blocks : blocks + 8] = jnp.ones((8, LANES), jnp.float32)
    weight[blocks : blocks + 8] = jnp.zeros((8, LANES), jnp.float32)

    spread = slot_relayout()
    for t in range(owners):
        rows = jnp.dot(spread, recv_ref[t], preferred_element_type=jnp.float32)
        table[8 * t : 8 * t + 8] = rows.reshape(8, 8, LANES)
    table[4 * slots : 4 * slots + 4] = jnp.zeros((4, 8, LANES), jnp.float32)

    def clear(t, carry):
        deposit[pl.ds(8 * t, 8)] = jnp.zeros((8, 8, LANES), jnp.float32)
        return carry

    lax.fori_loop(0, owners, clear, 0)
    deposit[4 * slots : 4 * slots + 4] = jnp.zeros((4, 8, LANES), jnp.float32)
    source[...] = jnp.zeros_like(source)
    to_scalar.wait()

    found = code_s[15, 0]
    for copy in copies:
        copy.wait()

    def entry(n0, i):
        code = code_s[n0 >> 7, (n0 & (LANES - 1)) + i]
        return code & (ENTRY - 1), code >> ENTRY_BITS

    cell_row = lax.broadcasted_iota(jnp.int32, (LANES, LANES), 0).astype(jnp.float32).astype(jnp.bfloat16)

    def look_up(j):
        n0 = STEP * j
        for i in range(0, STEP, 2):
            slot = entry(n0, i)[1]
            tile = [table[4 * slot + k] for k in range(ROWS_Y)]
            for h in range(2):
                b = entry(n0, i + h)[0]
                around = jnp.broadcast_to(cell[pl.ds(b, 1), :], (8, LANES))
                z, y = around & (LANES - 1), around >> 7
                rows = [jnp.take_along_axis(tile[k], z, axis=1) for k in range(ROWS_Y)]
                seen[i + h] = jnp.where(
                    y == 0, rows[0], jnp.where(y == 1, rows[1], jnp.where(y == 2, rows[2], rows[3]))
                )
                for k in range(3):
                    gathered[k, i + h : i + h + 1, :] = motion[k, pl.ds(b, 1), :]
                gathered[3, i + h : i + h + 1, :] = warmth[pl.ds(b, 1), :]
                gathered[4, i + h : i + h + 1, :] = mass[pl.ds(b, 1), :]
                gathered[5, i + h : i + h + 1, :] = weight[pl.ds(b, 1), :]

    def move():
        gas = [seen[:, f, :] for f in range(NF)]
        sources = coupling(
            gas,
            [gathered[k] for k in range(3)],
            gathered[3],
            gathered[4],
            gathered[5],
        )
        for f in range(NF):
            source[:, f, :] = sources[f]

    def scatter(j):
        n0 = STEP * j
        for i in range(0, STEP, 2):
            slot = entry(n0, i)[1]
            parts, hots = [], []
            for h in range(2):
                b = entry(n0, i + h)[0]
                cells = cell[pl.ds(b, 1), :]
                y = jnp.broadcast_to(cells, (8, LANES)) >> 7
                part = source[i + h]
                parts.append(
                    jnp.concatenate(
                        [jnp.where(y == k, part, 0.0) for k in range(ROWS_Y)], axis=0
                    ).astype(jnp.bfloat16)
                )
                hots.append(
                    jnp.where(cell_row == (cells & (LANES - 1)).astype(jnp.float32).astype(jnp.bfloat16), jnp.bfloat16(1), jnp.bfloat16(0))
                )
            added = lax.dot_general(
                jnp.concatenate(parts, axis=1),
                jnp.concatenate(hots, axis=1),
                NT,
                preferred_element_type=jnp.float32,
            ).reshape(4, 8, LANES)
            deposit[pl.ds(4 * slot, 4)] = deposit[pl.ds(4 * slot, 4)] + added

    def advance(j, carry):
        scatter(j)
        look_up(j + 1)
        move()
        return carry

    lax.fori_loop(0, (found + STEP - 1) // STEP + 1, advance, 0)

    back = slot_relayout_back()
    for t in range(owners):
        rows = deposit[8 * t : 8 * t + 8].reshape(64, LANES).astype(jnp.bfloat16)
        out_ref[t] = jnp.dot(back, rows, preferred_element_type=jnp.float32).astype(jnp.bfloat16)


def finish_kernel(
    planes,
    owners,
    holder_ref,
    flow_ref,
    nu_ref,
    xlo_ref,
    xhi_ref,
    up_ref,
    down_ref,
    landed_ref,
    out_ref,
    count,
    rows_above,
    rows_below,
):
    me = lax.axis_index("tile")
    g = lax.axis_index("grp")
    gas_groups = lax.axis_size("grp") - 1
    lane = lax.broadcasted_iota(jnp.int32, (ROWS_Y, LANES), 1)

    def clear(p, carry):
        count[p] = 0
        return carry

    lax.fori_loop(0, owners, clear, 0, unroll=True)

    rows_below[...] = up_ref[...].astype(jnp.float32)
    rows_above[...] = down_ref[...].astype(jnp.float32)
    xlo = [jnp.where(me > 0, xlo_ref[f], 0.0) for f in range(NF)]
    xhi = [jnp.where(me < owners - 1, xhi_ref[f], 0.0) for f in range(NF)]
    for x in range(planes):
        owner = holder_ref[x]
        rank = count[owner]
        count[owner] = rank + 1
        pair = landed_ref[owner].astype(jnp.float32)
        landed = jnp.where(rank == 0, pair[:HALF], pair[HALF : 2 * HALF])
        for f in range(NF):
            r = f * planes + x
            here = flow_ref[f, x]
            left = xlo[f] if x == 0 else flow_ref[f, x - 1]
            right = xhi[f] if x == planes - 1 else flow_ref[f, x + 1]
            first = jnp.where(g >= 1, rows_below[r : r + 1], 0.0)
            last = jnp.where(g < gas_groups - 1, rows_above[r : r + 1], 0.0)
            lower = jnp.concatenate([first, here[: ROWS_Y - 1]], axis=0)
            upper = jnp.concatenate([here[1:], last], axis=0)
            back = jnp.where(lane == 0, 0.0, pltpu.roll(here, 1, 1))
            ahead = jnp.where(lane == LANES - 1, 0.0, pltpu.roll(here, LANES - 1, 1))
            laplace = right + left + upper + lower + ahead + back - 6.0 * here
            value = here + 0.5 * nu_ref[x] * laplace + landed[ROWS_Y * f : ROWS_Y * f + ROWS_Y]
            out_ref[f, x] = jnp.where(g < gas_groups, value, 0.0)


def couple_call(live, pick, arrived, above, below, far, cell, motion, warmth, mass, weight):
    owners, blocks = arrived.shape[0], cell.shape[0]
    vmem = pl.BlockSpec(memory_space=pltpu.VMEM)
    smem = pl.BlockSpec(memory_space=pltpu.SMEM)
    hbm = pl.BlockSpec(memory_space=pl.ANY)
    params = pltpu.CompilerParams(vmem_limit_bytes=54336 * 1024)
    message = jax.ShapeDtypeStruct((owners, PAIR, LANES), jnp.bfloat16)

    def couple_body(*refs):
        couple_kernel(owners, blocks, *refs)

    return pl.pallas_call(
        couple_body,
        out_shape=message,
        in_specs=[smem] + [vmem] * 5 + [hbm] * 5,
        out_specs=vmem,
        scratch_shapes=[
            pltpu.VMEM((blocks + 8, LANES), jnp.int32),
            pltpu.VMEM((3, blocks + 8, LANES), jnp.float32),
            pltpu.VMEM((blocks + 8, LANES), jnp.float32),
            pltpu.VMEM((blocks + 8, LANES), jnp.float32),
            pltpu.VMEM((blocks + 8, LANES), jnp.float32),
            pltpu.VMEM((8 * owners + 4, 8, LANES), jnp.float32),
            pltpu.VMEM((8 * owners + 4, 8, LANES), jnp.float32),
            pltpu.VMEM((16, LANES), jnp.int32),
            pltpu.SMEM((16, LANES), jnp.int32),
            pltpu.VMEM((STEP, 8, LANES), jnp.float32),
            pltpu.VMEM((6, STEP, LANES), jnp.float32),
            pltpu.VMEM((STEP, 8, LANES), jnp.float32),
            pltpu.SemaphoreType.DMA((6,)),
        ],
        compiler_params=params,
    )(live, pick, arrived, above, below, far, cell, motion.transpose(1, 0, 2), warmth, mass, weight)


def local(
    flow_fields,
    turbulent_diffusivity,
    holder_unit,
    spray_volume_position,
    patch_pick_unreduced,
    droplet_motion,
    droplet_warmth,
    droplet_weightiness,
    droplet_multiplicity,
    living_spray_batches,
):
    groups = lax.axis_size("grp")
    owners = lax.axis_size("tile")
    planes = flow_fields.shape[1]
    blocks = spray_volume_position.shape[1]
    vmem = pl.BlockSpec(memory_space=pltpu.VMEM)
    smem = pl.BlockSpec(memory_space=pltpu.SMEM)
    params = pltpu.CompilerParams(vmem_limit_bytes=VMEM_LIMIT)

    holder = holder_unit.reshape(planes)

    def pack_body(*refs):
        pack_kernel(planes, owners, *refs)

    edge = jax.ShapeDtypeStruct((NF * planes, LANES), jnp.bfloat16)
    plane = jax.ShapeDtypeStruct((NF, ROWS_Y, LANES), jnp.float32)
    packed, top, bottom, front, behind = pl.pallas_call(
        pack_body,
        out_shape=(
            jax.ShapeDtypeStruct((owners, PAIR, LANES), jnp.bfloat16),
            edge,
            edge,
            plane,
            plane,
        ),
        in_specs=[smem, vmem],
        out_specs=(vmem,) * 5,
        scratch_shapes=[
            pltpu.SMEM((2 * owners,), jnp.int32),
            pltpu.SMEM((owners,), jnp.int32),
            pltpu.VMEM((NF * planes, LANES), jnp.float32),
            pltpu.VMEM((NF * planes, LANES), jnp.float32),
        ],
        compiler_params=params,
    )(holder, flow_fields)

    def turned(array, axis, step):
        size = lax.axis_size(axis)
        return lax.ppermute(array, axis, [(i, (i + step) % size) for i in range(size)])

    arrived = lax.all_to_all(packed, "tile", 0, 0, tiled=True)
    xlo = turned(behind, "tile", 1)
    xhi = turned(front, "tile", owners - 1)
    pick = patch_pick_unreduced.reshape(8, LANES).astype(jnp.float32)
    arrived, xlo, xhi, pick = lax.optimization_barrier((arrived, xlo, xhi, pick))

    held = (arrived[:, 0] < EMPTY).astype(jnp.float32) + (arrived[:, HALF] < EMPTY).astype(jnp.float32)
    number = jnp.broadcast_to(jnp.sum(held, axis=0), (8, LANES))
    above, far, below = (turned(number, "grp", k) for k in range(1, groups))

    outgoing = couple_call(
        living_spray_batches,
        pick,
        arrived,
        above,
        below,
        far,
        spray_volume_position[0],
        droplet_motion[0],
        droplet_warmth[0],
        droplet_weightiness[0],
        droplet_multiplicity[0],
    )

    outgoing, top, bottom = lax.optimization_barrier((outgoing, top, bottom))
    landed = lax.all_to_all(outgoing, "tile", 0, 0, tiled=True)
    up = turned(top, "grp", 1)
    down = turned(bottom, "grp", groups - 1)

    def finish_body(*refs):
        finish_kernel(planes, owners, *refs)

    return pl.pallas_call(
        finish_body,
        out_shape=jax.ShapeDtypeStruct(flow_fields.shape, jnp.float32),
        in_specs=[smem] + [vmem] * 7,
        out_specs=vmem,
        scratch_shapes=[
            pltpu.SMEM((owners,), jnp.int32),
            pltpu.VMEM((NF * planes, LANES), jnp.float32),
            pltpu.VMEM((NF * planes, LANES), jnp.float32),
        ],
        compiler_params=pltpu.CompilerParams(vmem_limit_bytes=40 * 1024 * 1024),
    )(holder, flow_fields, turbulent_diffusivity, xlo, xhi, up, down, landed)


def solution(mesh):
    in_specs = (
        P(None, "tile", "grp", None),
        P("tile", "grp", None),
        P("grp", "tile", None),
        P("tile", None, None),
        P("tile", None),
        P("tile", None, None, None),
        P("tile", None, None),
        P("tile", None, None),
        P("tile", None, None),
        P("tile"),
    )
    out_specs = P(None, "tile", "grp", None)
    return jax.shard_map(local, mesh=mesh, in_specs=in_specs, out_specs=out_specs, check_vma=False)
```
